256 devices in a mesh: ctx: 32 (over x, z), head: 8 (over y, core).
Axes of the slice: x: 4, y: 4, z: 8, core: 2. Of those that a mesh axis runs over, the one named last changes fastest.
Arguments:
- queries: bfloat16 [8192, 4096], P('ctx', 'head'), may hold values from -6 to 6
- keys: bfloat16 [8192, 4096], P('ctx', 'head'), may hold values from -6 to 6
- values: bfloat16 [8192, 4096], P('ctx', 'head'), may hold values from -24 to 24
- upstream: bfloat16 [8192, 4096], P('ctx', 'head'), may hold values from -12 to 12
- out_weight: bfloat16 [4096, 4096], P('head'), may hold values from -0.09375 to 0.09375
Outputs:
- attention: bfloat16 [8192, 4096], P('ctx', 'head')
- grad_queries: bfloat16 [8192, 4096], P('ctx', 'head')
- grad_keys: bfloat16 [8192, 4096], P('ctx', 'head')
- grad_values: bfloat16 [8192, 4096], P('ctx', 'head')
- wo_grad: float32 [4096, 4096], P('ctx', 'head')
The draws below stay inside these ranges and needn't reach their ends.
All inputs are finite; a program needn't handle non-finite values.
Results may differ from the reference program's by a relative error of at most 0.023.
Values may be sent and summed in bfloat16 or wider, within the bound.
A program may use at most 128 MiB of HBM per device.

```python
import math
import jax
import jax.numpy as jnp
from jax import lax

D = 4096
HEADS = 32
HDIM = 128
BLK = 256
LEVELS = 5
TOKENS = 8192


def drawn_pair(base_key):
    folded = jax.random.fold_in(base_key, 11)
    query_key, keys_key = jax.random.split(folded, 2)
    full_shape = (TOKENS // BLK, BLK, HEADS, HDIM)
    query_part = jax.random.truncated_normal(query_key, -6.0, 6.0, full_shape, jnp.float32)
    key_part = jax.random.truncated_normal(keys_key, -6.0, 6.0, full_shape, jnp.float32)
    return (query_part.reshape(TOKENS, HEADS * HDIM), key_part.reshape(TOKENS, HEADS * HDIM))


def draw_queries(key, part):
    return drawn_pair(key)[0].astype(jnp.bfloat16)


def draw_keys(key, part):
    return drawn_pair(key)[1].astype(jnp.bfloat16)


def raised(drawn, rng, source, target, blocks, factor):
    owner, partner = [(jnp.arange(drawn.shape[axis_at]) // (drawn.shape[axis_at] // blocks)).reshape([-1 if axis == axis_at else 1 for axis in range(drawn.ndim)]) for axis_at in (source, target)]
    chosen = jax.random.permutation(rng, blocks)[partner]
    strong = (owner == chosen) | (owner == (partner + blocks // 2) % blocks)
    return jnp.where(strong, factor * drawn, drawn)


def block_levels(stream_key, extent, cuts, smallest, top_value):
    def one(dim, shards_of):
        heights = jax.random.uniform(jax.random.fold_in(jax.random.fold_in(stream_key, 6), dim), (shards_of,), jnp.float32, smallest / len(cuts), top_value / len(cuts))
        return jnp.repeat(jnp.exp(heights), extent[dim] // shards_of).reshape((-1,) + (1,) * (len(extent) - dim - 1))

    level = one(*cuts[0])
    for cut in cuts[1:]:
        level = level * one(*cut)
    return level


def noise(stream_key, extent, spread, bound, pieces=(), held_as=jnp.bfloat16):
    factor_of = block_levels(stream_key, extent, pieces, -0.22, 0.18) if pieces else 1.0
    values = jax.random.normal(stream_key, extent, jnp.float32) * spread * factor_of
    return jnp.minimum(jnp.maximum(values, -bound), bound).astype(held_as)


def gaussian_with(rng, shape, scale, most, pieces, heavy, kind=jnp.bfloat16):
    values = scale * jax.random.normal(rng, shape, jnp.float32)
    if pieces:
        values = values * block_levels(rng, shape, pieces, -0.22, 0.18)
    return jnp.clip(raised(values, jax.random.fold_in(rng, 3), *heavy), -most, most).astype(kind)


def setup_inputs(seed: int = 0) -> dict:
    arg_keys = jax.random.split(jax.random.key(seed), 6)
    return {
        "queries": draw_queries(jax.random.fold_in(arg_keys[5], 71), 0),
        "keys": draw_keys(jax.random.fold_in(arg_keys[5], 71), 0),
        "values": noise(arg_keys[2], (TOKENS, HEADS * HDIM), 4.0, 24.0, ((0, 32), (1, 8))),
        "upstream": gaussian_with(arg_keys[3], (TOKENS, D), 2.0, 12.0, ((0, 32), (1, 8)), (0, 1, 32, 2.75)),
        "out_weight": noise(arg_keys[4], (HEADS * HDIM, D), (HEADS * HDIM) ** -0.5, 0.09375, ((0, 8),)),
    }


def level_distances():
    return [0] + [2 ** level for level in range(LEVELS)]

def per_head(tensor):
    block_count = tensor.shape[0] // BLK
    return tensor.reshape(block_count, BLK, HEADS, HDIM).transpose(2, 0, 1, 3)

def from_heads(tensor):
    return tensor.transpose(1, 2, 0, 3).reshape(-1, HEADS * HDIM)

def stack_levels(tensor):
    block_count = tensor.shape[0]
    layers = []
    for distance in level_distances():
        padded = jnp.concatenate([jnp.zeros((distance,) + tensor.shape[1:], tensor.dtype), tensor], 0)
        layers.append(padded[:block_count])
    return jnp.stack(layers)

def unstack_levels(gradients):
    block_count = gradients.shape[1]
    result = jnp.zeros(gradients.shape[1:], jnp.float32)
    for level_index, distance in enumerate(level_distances()):
        padded = jnp.concatenate([gradients[level_index], jnp.zeros((distance,) + gradients.shape[2:], gradients.dtype)], 0)
        result = result + padded[distance:distance + block_count]
    return result

def level_mask(block_count):
    block_ids = jnp.arange(block_count)
    valid = jnp.stack([block_ids >= distance for distance in level_distances()], 1)
    row_ids = jnp.arange(BLK)
    causal = row_ids[:, None] >= row_ids[None, :]
    within = jnp.concatenate([causal[None], jnp.ones((LEVELS, BLK, BLK), jnp.bool_)], 0)
    return valid[:, :, None, None] & within[None]

def softmax_parts(query_rows, key_stack, visible):
    scaling = 1.0 / math.sqrt(HDIM)
    scores = jnp.einsum('nqd,lnkd->nlqk', query_rows.astype(jnp.float32), key_stack.astype(jnp.float32)) * scaling
    row_max = lax.optimization_barrier(jnp.max(jnp.where(visible, scores, -jnp.inf), axis=(1, 3)))
    weights = jnp.where(visible, jnp.exp(scores - row_max[:, None, :, None]), 0.0)
    totals = lax.optimization_barrier(jnp.sum(weights, axis=(1, 3)))
    return (weights, totals)

def rounded(tensor):
    return lax.optimization_barrier(tensor.astype(jnp.bfloat16)).astype(jnp.float32)

def reference(queries, keys, values, upstream, out_weight):
    block_count = queries.shape[0] // BLK
    visible = level_mask(block_count)
    scaling = 1.0 / math.sqrt(HDIM)

    def forward_head(inputs):
        query_rows, key_rows, value_rows = inputs
        key_stack = stack_levels(key_rows)
        value_stack = stack_levels(value_rows)
        weights, totals = softmax_parts(query_rows, key_stack, visible)
        mixed = jnp.einsum('nlqk,lnkd->nqd', rounded(weights), value_stack.astype(jnp.float32))
        return (mixed / totals[:, :, None]).astype(jnp.bfloat16)
    attention = from_heads(lax.map(forward_head, (per_head(queries), per_head(keys), per_head(values))))
    context_grad = jnp.dot(upstream, out_weight.T, preferred_element_type=jnp.float32).astype(jnp.bfloat16)
    wo_grad = jnp.dot(upstream.T, attention, preferred_element_type=jnp.float32)

    def backward_head(inputs):
        query_rows, key_rows, value_rows, output, out_grad = inputs
        key_stack = stack_levels(key_rows)
        value_stack = stack_levels(value_rows)
        weights, totals = softmax_parts(query_rows, key_stack, visible)
        normed = weights / totals[:, None, :, None]
        out_gradf = out_grad.astype(jnp.float32)
        row_dots = lax.optimization_barrier(jnp.sum(out_gradf * output.astype(jnp.float32), -1))
        value_grads = jnp.einsum('nlqk,nqd->lnkd', rounded(normed), out_gradf)
        prob_grad = jnp.einsum('nqd,lnkd->nlqk', out_gradf, value_stack.astype(jnp.float32))
        score_grad = rounded(normed * (prob_grad - row_dots[:, None, :, None]))
        query_grad = (scaling * jnp.einsum('nlqk,lnkd->nqd', score_grad, key_stack.astype(jnp.float32))).astype(jnp.bfloat16)
        key_grads = scaling * jnp.einsum('nlqk,nqd->lnkd', score_grad, query_rows.astype(jnp.float32))
        return (query_grad, unstack_levels(key_grads).astype(jnp.bfloat16), unstack_levels(value_grads).astype(jnp.bfloat16))
    gradients = lax.map(backward_head, (per_head(queries), per_head(keys), per_head(values), per_head(attention), per_head(context_grad)))
    return (attention, from_heads(gradients[0]), from_heads(gradients[1]), from_heads(gradients[2]), wo_grad)
```

```python
import functools
import math

import jax
import jax.numpy as jnp
from jax import lax
from jax.experimental import pallas as pl
from jax.experimental.pallas import tpu as pltpu
from jax.sharding import PartitionSpec as P

HDIM = 128
BLK = 256
DISTANCES = (0, 1, 2, 4, 8, 16)
LV = len(DISTANCES)
HEADS = 4
FEAT = HEADS * HDIM
D = 4096
CTX = 32
ZS = 8
XS = 4
HP = 8
SCALING = 1.0 / math.sqrt(HDIM)
MESH = pl.DeviceIdType.MESH
BF16 = jnp.bfloat16
F32 = jnp.float32

KV_ROUTE = {1: (0, 1), 2: (1, 1), 3: (2, 2), 4: (0, 8), 5: (4, 8)}


def wrap(i, n):
    return lax.rem(i + n, n)


def dot_nt(a, b):
    return lax.dot_general(a, b, (((1,), (1,)), ((), ())), preferred_element_type=F32)


def dot_nn(a, b):
    return lax.dot_general(a, b, (((1,), (0,)), ((), ())), preferred_element_type=F32)


def dot_tn(a, b):
    return lax.dot_general(a, b, (((0,), (0,)), ((), ())), preferred_element_type=F32)


def kernel(
    q_in, k_in, v_in, up_in, w_in,
    att_o, dq_o, dk_o, dv_o, wo_o,
    kv, qh, fu, wv, uu, cg_acc, cgh, sc, nb, att_all, own, gs, gr, wos, wor,
    loc, kv_s, kv_r, gr_s, gr_r, fu_s, fu_r, ua_s, ua_r, ug_s, ug_r, at_s, at_r, wo_s, wo_r,
):
    c = lax.axis_index("ctx")
    h = lax.axis_index("head")
    x = lax.div(c, ZS)
    z = lax.rem(c, ZS)
    owns = lax.rem(c, XS) == x

    def at_ctx(shift):
        return (lax.rem(c + (shift + CTX), CTX), h)

    def at_head(shift):
        return (c, lax.rem(h + shift, HP))

    def cols(j, width):
        return pl.ds(pl.multiple_of(j * width, 128), width)

    def local_copy(i):
        kind, j = divmod(i, HEADS)
        src = (k_in, v_in, q_in)[kind].at[:, j * HDIM : (j + 1) * HDIM]
        dst = qh.at[j] if kind == 2 else kv.at[j, kind, 0]
        return pltpu.make_async_copy(src, dst, loc.at[i])

    up_copy = pltpu.make_async_copy(up_in, fu.at[h], loc.at[12])
    piece_copy = pltpu.make_async_copy(up_in.at[:, cols(x, HDIM)], uu.at[h, x], loc.at[13])
    w_copy = pltpu.make_async_copy(w_in, wv, loc.at[14])

    def kv_copy(lv, j):
        src, shift = KV_ROUTE[lv]
        return pltpu.make_async_remote_copy(
            kv.at[j, :, src], kv.at[j, :, lv], kv_s.at[lv - 1, j], kv_r.at[lv - 1, j],
            device_id=at_ctx(shift), device_id_type=MESH)

    def gr_copy(lv, j):
        shift = KV_ROUTE[lv][1]
        return pltpu.make_async_remote_copy(
            gs.at[lv - 1, j], gr.at[lv - 1, j], gr_s.at[lv - 1, j], gr_r.at[lv - 1, j],
            device_id=at_ctx(-shift), device_id_type=MESH)

    def fu_copy(s):
        return pltpu.make_async_remote_copy(
            up_in, fu.at[h], fu_s.at[s], fu_r.at[s], device_id=at_head(s), device_id_type=MESH)

    def ua_copy(s):
        target = lax.rem(x + s, XS)
        return pltpu.make_async_remote_copy(
            up_in.at[:, cols(target, HDIM)], uu.at[h, x], ua_s.at[s], ua_r.at[s],
            device_id=at_ctx(s * ZS), device_id_type=MESH)

    def ug_copy(s):
        return pltpu.make_async_remote_copy(
            uu.at[h], uu.at[h], ug_s.at[s], ug_r.at[s], device_id=at_head(s), device_id_type=MESH)

    def at_copy(s, j):
        part = att_all.at[x, :, cols(j, HDIM)]
        return pltpu.make_async_remote_copy(
            part, part, at_s.at[s, j], at_r.at[s, j], device_id=at_ctx(s * ZS), device_id_type=MESH)

    def wo_copy(i):
        return pltpu.make_async_remote_copy(
            wos.at[i], wor.at[z], wo_s.at[i], wo_r.at[z], device_id=(XS * i + x, h),
            device_id_type=MESH)

    def wo_arrival(i):
        return pltpu.make_async_remote_copy(
            wos.at[i], wor.at[i], wo_s.at[i], wo_r.at[i], device_id=(XS * i + x, h),
            device_id_type=MESH)

    for i in range(12):
        local_copy(i).start()
    up_copy.start()
    piece_copy.start()
    w_copy.start()

    barrier = pltpu.get_barrier_semaphore()
    for shift in (1, 2, -1, -2, 8, 16, 24):
        pl.semaphore_signal(barrier, inc=1, device_id=at_ctx(shift), device_id_type=MESH)
    for s in range(1, HP):
        pl.semaphore_signal(barrier, inc=1, device_id=at_head(s), device_id_type=MESH)

    def greet(i, carry):
        sender = ZS * lax.rem(c, XS) + i

        @pl.when(sender != c)
        def _():
            pl.semaphore_signal(barrier, inc=1, device_id=(sender, h), device_id_type=MESH)

        return carry

    lax.fori_loop(0, ZS, greet, 0)

    @pl.when(owns)
    def _():
        pl.semaphore_wait(barrier, 21)

    @pl.when(jnp.logical_not(owns))
    def _():
        pl.semaphore_wait(barrier, 22)

    for j in range(HEADS):
        local_copy(j).wait()
        local_copy(HEADS + j).wait()
        kv_copy(1, j).start()
        kv_copy(4, j).start()
    for s in range(1, XS):
        ua_copy(s).start()
    for s in range(1, HP):
        fu_copy(s).start()

    def relay_one(j, carry):
        kv_copy(1, j).wait_recv()
        kv_copy(2, j).start()
        kv_copy(4, j).wait_recv()
        kv_copy(5, j).start()
        return carry

    lax.fori_loop(0, HEADS, relay_one, 0)
    piece_copy.wait()
    for s in range(1, XS):
        ua_copy(s).wait_recv()
    for s in range(1, HP):
        ug_copy(s).start()

    def relay_two(j, carry):
        kv_copy(2, j).wait_recv()
        kv_copy(3, j).start()
        return carry

    lax.fori_loop(0, HEADS, relay_two, 0)

    w_copy.wait()
    up_copy.wait()
    cg_acc[...] = dot_nt(fu[h], wv[:, cols(h, FEAT)])

    def context_step(s, carry):
        fu_copy(s).wait_recv()
        peer = lax.rem(h + (HP - s), HP)
        cg_acc[...] += dot_nt(fu[peer], wv[:, cols(peer, FEAT)])
        return carry

    lax.fori_loop(1, HP, context_step, 0)
    for j in range(HEADS):
        cgh[j] = cg_acc[:, j * HDIM : (j + 1) * HDIM].astype(BF16)
        local_copy(2 * HEADS + j).wait()

    def head(j):
        kv_copy(3, j).wait_recv()
        kv_copy(5, j).wait_recv()
        q = qh[j]
        cg = cgh[j]
        row_max = None
        for lv in range(LV):
            s = dot_nt(kv[j, 0, lv], q) * SCALING
            if lv == 0:
                key_id = lax.broadcasted_iota(jnp.int32, (BLK, BLK), 0)
                query_id = lax.broadcasted_iota(jnp.int32, (BLK, BLK), 1)
                s = jnp.where(key_id <= query_id, s, -1e30)
            else:
                s = s + jnp.where(c >= DISTANCES[lv], 0.0, -1e30).astype(F32)
            sc[lv] = s
            top = jnp.max(s, axis=0, keepdims=True)
            row_max = top if row_max is None else jnp.maximum(row_max, top)
        totals = jnp.zeros((1, BLK), F32)
        for lv in range(LV):
            w = jnp.exp(sc[lv] - row_max)
            sc[lv] = w
            totals = totals + jnp.sum(w, axis=0, keepdims=True)
            nb[lv * BLK : (lv + 1) * BLK, :] = w.astype(BF16)
        inverse = 1.0 / totals
        mixed = dot_tn(kv[j, 1].reshape(LV * BLK, HDIM), nb[...])
        att_t = (mixed * inverse).astype(BF16).astype(F32)
        att = att_t.T.astype(BF16)
        att_o[:, cols(j, HDIM)] = att
        att_all[x, :, cols(j, HDIM)] = att
        for s in range(1, XS):
            at_copy(s, j).start()
        row_dots = jnp.sum(cg.astype(F32).T * att_t, axis=0, keepdims=True)
        for lv in range(LV):
            normed = sc[lv] * inverse
            prob_grad = dot_nt(kv[j, 1, lv], cg)
            ds = (normed * (prob_grad - row_dots)).astype(BF16)
            nb[lv * BLK : (lv + 1) * BLK, :] = ds
            dv = dot_nn(normed.astype(BF16), cg)
            dk = dot_nn(ds, q) * SCALING
            if lv in (3, 5):
                gs[lv - 1, j, 0] = dk.astype(BF16)
                gs[lv - 1, j, 1] = dv.astype(BF16)
                gr_copy(lv, j).start()
            else:
                own[lv, j, 0] = dk
                own[lv, j, 1] = dv
        dq_t = dot_tn(kv[j, 0].reshape(LV * BLK, HDIM), nb[...]) * SCALING
        dq_o[:, cols(j, HDIM)] = dq_t.T.astype(BF16)

    def pass_on(src, dst, j):
        gr_copy(src, j).wait_recv()
        gs[dst - 1, j] = (own[dst, j] + gr[src - 1, j].astype(F32)).astype(BF16)
        gr_copy(dst, j).start()

    def stage(t, do_head):
        if do_head:
            head(t)

        @pl.when((t >= 1) & (t < HEADS + 1))
        def _():
            pass_on(3, 2, t - 1)
            pass_on(5, 4, t - 1)

        @pl.when((t >= 2) & (t < HEADS + 2))
        def _():
            pass_on(2, 1, t - 2)

        @pl.when(t >= 3)
        def _():
            j = t - 3
            gr_copy(1, j).wait_recv()
            gr_copy(4, j).wait_recv()
            total = own[0, j] + gr[0, j].astype(F32) + gr[3, j].astype(F32)
            dk_o[:, cols(j, HDIM)] = total[0].astype(BF16)
            dv_o[:, cols(j, HDIM)] = total[1].astype(BF16)

    def stage_head(t, carry):
        stage(t, True)
        return carry

    def stage_tail(t, carry):
        stage(t, False)
        return carry

    lax.fori_loop(0, HEADS, stage_head, 0)

    for s in range(1, XS):
        for j in range(HEADS):
            at_copy(s, j).wait_recv()
    for s in range(1, HP):
        ug_copy(s).wait_recv()

    def project(n, carry):
        i = lax.rem(z + n, HP)
        part = dot_tn(
            uu[i].reshape(XS * BLK, HDIM), att_all[...].reshape(XS * BLK, FEAT)
        ).astype(BF16)

        @pl.when(XS * i + x != c)
        def _():
            wos[i] = part
            wo_copy(i).start()

        @pl.when(XS * i + x == c)
        def _():
            wor[z] = part

        return carry

    lax.fori_loop(0, HP, project, 0)

    lax.fori_loop(HEADS, HEADS + 3, stage_tail, 0)

    wo_o[...] = jnp.zeros((HDIM, FEAT), F32)

    def gather(i, carry):
        @pl.when(ZS * lax.rem(c, XS) + i != c)
        def _():
            wo_arrival(i).wait_recv()

        wo_o[...] += wor[i].astype(F32)
        return carry

    lax.fori_loop(0, ZS, gather, 0)

    def drain(j, carry):
        for lv in range(1, LV):
            kv_copy(lv, j).wait_send()
            gr_copy(lv, j).wait_send()
        for s in range(1, XS):
            at_copy(s, j).wait_send()
        return carry

    lax.fori_loop(0, HEADS, drain, 0)
    for s in range(1, XS):
        ua_copy(s).wait_send()
    for s in range(1, HP):
        fu_copy(s).wait_send()
        ug_copy(s).wait_send()

    def drain_wo(i, carry):
        @pl.when(XS * i + x != c)
        def _():
            wo_copy(i).wait_send()

        return carry

    lax.fori_loop(0, HP, drain_wo, 0)


def per_device(queries, keys, values, upstream, out_weight):
    tokens = jax.ShapeDtypeStruct((BLK, FEAT), BF16)
    dma = pltpu.SemaphoreType.DMA
    vmem = pltpu.VMEM
    return pl.pallas_call(
        kernel,
        out_shape=(tokens, tokens, tokens, tokens, jax.ShapeDtypeStruct((HDIM, FEAT), F32)),
        in_specs=[pl.BlockSpec(memory_space=pl.ANY)] * 5,
        out_specs=(pl.BlockSpec(memory_space=pltpu.VMEM),) * 5,
        scratch_shapes=[
            vmem((HEADS, 2, LV, BLK, HDIM), BF16),
            vmem((HEADS, BLK, HDIM), BF16),
            vmem((HP, BLK, FEAT), BF16),
            vmem((FEAT, D), BF16),
            vmem((HP, XS, BLK, HDIM), BF16),
            vmem((BLK, FEAT), F32),
            vmem((HEADS, BLK, HDIM), BF16),
            vmem((LV, BLK, BLK), F32),
            vmem((LV * BLK, BLK), BF16),
            vmem((XS, BLK, FEAT), BF16),
            vmem((5, HEADS, 2, BLK, HDIM), F32),
            vmem((5, HEADS, 2, BLK, HDIM), BF16),
            vmem((5, HEADS, 2, BLK, HDIM), BF16),
            vmem((HP, HDIM, FEAT), BF16),
            vmem((ZS, HDIM, FEAT), BF16),
            dma((15,)),
            dma((5, HEADS)), dma((5, HEADS)),
            dma((5, HEADS)), dma((5, HEADS)),
            dma((HP,)), dma((HP,)),
            dma((XS,)), dma((XS,)),
            dma((HP,)), dma((HP,)),
            dma((XS, HEADS)), dma((XS, HEADS)),
            dma((HP,)), dma((ZS,)),
        ],
        compiler_params=pltpu.CompilerParams(
            collective_id=0, has_side_effects=True, vmem_limit_bytes=56 * 1024 * 1024
        ),
        cost_estimate=pl.CostEstimate(flops=5 * 10**9, bytes_accessed=10**7, transcendentals=2 * 10**6),
        name="log_sparse_attention",
    )(queries, keys, values, upstream, out_weight)


def solution(mesh):
    tiled = P("ctx", "head")
    return jax.shard_map(
        per_device,
        mesh=mesh,
        in_specs=(tiled, tiled, tiled, tiled, P("head", None)),
        out_specs=(tiled,) * 5,
        check_vma=False,
    )
```

```python
import math

import jax
import jax.numpy as jnp
from jax import lax
from jax.experimental import pallas as pl
from jax.experimental.pallas import tpu as pltpu
from jax.sharding import PartitionSpec as P

HDIM = 128
BLK = 256
DISTANCES = (0, 1, 2, 4, 8, 16)
LV = len(DISTANCES)
HEADS = 4
FEAT = HEADS * HDIM
D = 4096
CTX = 32
ZS = 8
XS = 4
HP = 8
SCALING = 1.0 / math.sqrt(HDIM)
MESH = pl.DeviceIdType.MESH
BF16 = jnp.bfloat16
F32 = jnp.float32

KV_ROUTE = {1: (0, 1), 2: (1, 1), 3: (2, 2), 4: (0, 8), 5: (4, 8)}


def dot_nt(a, b):
    return lax.dot_general(a, b, (((1,), (1,)), ((), ())), preferred_element_type=F32)


def dot_nn(a, b):
    return lax.dot_general(a, b, (((1,), (0,)), ((), ())), preferred_element_type=F32)


def dot_tn(a, b):
    return lax.dot_general(a, b, (((0,), (0,)), ((), ())), preferred_element_type=F32)


def kernel(
    q_in, k_in, v_in, up_in, w_in,
    att_o, dq_o, dk_o, dv_o, wo_o,
    kv, qh, fu, wv, ust, uu, cg_acc, cgh, sc, nb, att_all, own, gs, gr, wos, wor,
    loc, kv_s, kv_r, gr_s, gr_r, fy_s, fy_r, fc_s, fc_r, ua_s, ua_r, uy_s, uy_r, uc_s, uc_r,
    at_s, at_r, wo_s, wo_r,
):
    c = lax.axis_index("ctx")
    h = lax.axis_index("head")
    x = lax.div(c, ZS)
    z = lax.rem(c, ZS)
    core = lax.rem(h, 2)
    twin = h + 1 - 2 * core

    def at_ctx(shift):
        return (lax.rem(c + (shift + CTX), CTX), h)

    def at_z(shift):
        return (x * ZS + lax.rem(z + (shift + ZS), ZS), h)

    def at_head(shift):
        return (c, lax.rem(h + shift, HP))

    def cols(j, width):
        return pl.ds(pl.multiple_of(j * width, 128), width)

    def remote(src, dst, send, recv, device):
        return pltpu.make_async_remote_copy(
            src, dst, send, recv, device_id=device, device_id_type=MESH)

    def local_copy(kind, j):
        src = (k_in, v_in, q_in)[kind].at[:, j * HDIM : (j + 1) * HDIM]
        dst = qh.at[j] if kind == 2 else kv.at[j, kind, 0]
        return pltpu.make_async_copy(src, dst, loc.at[kind * HEADS + j])

    up_copy = pltpu.make_async_copy(up_in, fu.at[h], loc.at[12])
    w_copy = pltpu.make_async_copy(w_in, wv, loc.at[13])

    def kv_copy(lv, j, src=None):
        route, shift = KV_ROUTE[lv]
        return remote(
            kv.at[j, :, route if src is None else src], kv.at[j, :, lv],
            kv_s.at[lv - 1, j], kv_r.at[lv - 1, j], at_z(1) if lv == 1 else at_ctx(shift))

    def gr_copy(lv, j):
        return remote(
            gs.at[lv - 1, j], gr.at[lv - 1, j], gr_s.at[lv - 1, j], gr_r.at[lv - 1, j],
            at_ctx(-KV_ROUTE[lv][1]))

    def from_y(s):
        return lax.rem(h + (HP - 2 * s), HP)

    def fy_copy(s):
        return remote(up_in, fu.at[h], fy_s.at[s], fy_r.at[s], at_head(2 * s))

    def fc_copy(s):
        slot = from_y(s)
        return remote(up_in if s == 0 else fu.at[slot], fu.at[slot], fc_s.at[s], fc_r.at[s], (c, twin))

    def ua_copy(s):
        return remote(ust.at[s], uu.at[h, x], ua_s.at[s], ua_r.at[s], at_ctx(s * ZS))

    def uy_copy(s):
        return remote(uu.at[h], uu.at[h], uy_s.at[s], uy_r.at[s], at_head(2 * s))

    def uc_copy(s):
        slot = from_y(s)
        return remote(uu.at[slot], uu.at[slot], uc_s.at[s], uc_r.at[s], (c, twin))

    def at_copy(s, j):
        part = att_all.at[x, j]
        return remote(part, part, at_s.at[s, j], at_r.at[s, j], at_ctx(s * ZS))

    def wo_copy(n, j):
        return remote(wos.at[n, j], wor.at[z, j], wo_s.at[n, j], wo_r.at[n, j], at_z(n))

    for j in range(HEADS):
        local_copy(0, j).start()
        local_copy(1, j).start()
    up_copy.start()
    for j in range(HEADS):
        local_copy(2, j).start()
    w_copy.start()

    barrier = pltpu.get_barrier_semaphore()
    peers = [at_ctx(shift) for shift in (1, -1, 2, -2, 8, 16, 24)]
    peers += [at_head(s) for s in (2, 4, 6)] + [(c, twin)]
    peers += [at_z(s) for s in range(1, ZS)]
    for peer in peers:
        pl.semaphore_signal(barrier, inc=1, device_id=peer, device_id_type=MESH)
    pl.semaphore_wait(barrier, len(peers))

    for j in range(HEADS):
        local_copy(0, j).wait()
        local_copy(1, j).wait()
        if j < 2:
            @pl.when(z < ZS - 1)
            def _():
                kv_copy(1, j).start()
        kv_copy(4, j).start()
        if j == 0:
            fc_copy(0).start()
            for s in range(1, XS):
                fy_copy(s).start()

    def relay(j):
        kv_copy(4, j).wait_recv()
        kv_copy(5, j).start()

        @pl.when(z == ZS - 1)
        def _():
            kv_copy(1, j, 4).start()

        kv_copy(1, j).wait_recv()
        kv_copy(2, j).start()

        @pl.when((j < HEADS - 2) & (z < ZS - 1))
        def _():
            kv_copy(1, j + 2).start()

        kv_copy(2, j).wait_recv()
        kv_copy(3, j).start()

    def context():
        for s in range(1, XS):
            fy_copy(s).wait_recv()
            fc_copy(s).start()
        w_copy.wait()
        up_copy.wait()
        cg_acc[...] = dot_nt(fu[h], wv[:, cols(h, FEAT)])

        def add_tile(tile):
            cg_acc[...] += dot_nt(fu[tile], wv[:, cols(tile, FEAT)])

        def near(s, carry):
            add_tile(lax.rem(h + (HP - 2 * s), HP))
            return carry

        lax.fori_loop(1, XS, near, 0)
        for s in range(XS):
            fc_copy(s).wait_recv()

        def twins(s, carry):
            add_tile(lax.rem(twin + (HP - 2 * s), HP))
            return carry

        lax.fori_loop(0, XS, twins, 0)
        for j in range(HEADS):
            cgh[j] = cg_acc[:, j * HDIM : (j + 1) * HDIM].astype(BF16)
            local_copy(2, j).wait()
        for s in range(XS):
            target = lax.rem(x + s, XS)
            tile = fu[2 * target + lax.div(h, 4), :, cols(lax.rem(h, 4), HDIM)].T
            if s == 0:
                uu[h, x] = tile
            else:
                ust[s] = tile
                ua_copy(s).start()

    def spread_columns():
        for s in range(1, XS):
            ua_copy(s).wait_recv()
        uc_copy(0).start()
        for s in range(1, XS):
            uy_copy(s).start()

    def finish_columns():
        for s in range(1, XS):
            uy_copy(s).wait_recv()
            uc_copy(s).start()
        for s in range(XS):
            uc_copy(s).wait_recv()

    def head(j):
        kv_copy(3, j).wait_recv()
        kv_copy(5, j).wait_recv()
        q = qh[j]
        cg = cgh[j]
        row_max = None
        for lv in range(LV):
            s = dot_nt(kv[j, 0, lv], q) * SCALING
            if lv == 0:
                key_id = lax.broadcasted_iota(jnp.int32, (BLK, BLK), 0)
                query_id = lax.broadcasted_iota(jnp.int32, (BLK, BLK), 1)
                s = jnp.where(key_id <= query_id, s, -1e30)
            else:
                s = s + jnp.where(c >= DISTANCES[lv], 0.0, -1e30).astype(F32)
            sc[lv] = s
            top = jnp.max(s, axis=0, keepdims=True)
            row_max = top if row_max is None else jnp.maximum(row_max, top)
        totals = jnp.zeros((1, BLK), F32)
        for lv in range(LV):
            w = jnp.exp(sc[lv] - row_max)
            sc[lv] = w
            totals = totals + jnp.sum(w, axis=0, keepdims=True)
            nb[lv * BLK : (lv + 1) * BLK, :] = w.astype(BF16)
        inverse = 1.0 / totals
        mixed = dot_tn(kv[j, 1].reshape(LV * BLK, HDIM), nb[...])
        att_t = (mixed * inverse).astype(BF16).astype(F32)
        att = att_t.T.astype(BF16)
        att_o[:, cols(j, HDIM)] = att
        att_all[x, j] = att
        for s in range(1, XS):
            at_copy(s, j).start()
        row_dots = jnp.sum(cg.astype(F32).T * att_t, axis=0, keepdims=True)
        for lv in range(LV):
            normed = sc[lv] * inverse
            prob_grad = dot_nt(kv[j, 1, lv], cg)
            ds = (normed * (prob_grad - row_dots)).astype(BF16)
            nb[lv * BLK : (lv + 1) * BLK, :] = ds
            dv = dot_nn(normed.astype(BF16), cg)
            dk = dot_nn(ds, q) * SCALING
            if lv in (3, 5):
                gs[lv - 1, j, 0] = dk.astype(BF16)
                gs[lv - 1, j, 1] = dv.astype(BF16)
                gr_copy(lv, j).start()
            else:
                own[lv, j, 0] = dk
                own[lv, j, 1] = dv
        dq_t = dot_tn(kv[j, 0].reshape(LV * BLK, HDIM), nb[...]) * SCALING
        dq_o[:, cols(j, HDIM)] = dq_t.T.astype(BF16)

    def pass_on(src, dst, j):
        gr_copy(src, j).wait_recv()
        gs[dst - 1, j] = (own[dst, j] + gr[src - 1, j].astype(F32)).astype(BF16)
        gr_copy(dst, j).start()

    def chain_one(j):
        pass_on(3, 2, j)
        pass_on(5, 4, j)

    def chain_two(j):
        pass_on(2, 1, j)

    def last(j):
        gr_copy(1, j).wait_recv()
        gr_copy(4, j).wait_recv()
        total = own[0, j] + gr[0, j].astype(F32) + gr[3, j].astype(F32)
        dk_o[:, cols(j, HDIM)] = total[0].astype(BF16)
        dv_o[:, cols(j, HDIM)] = total[1].astype(BF16)

    def project(j):
        for s in range(1, XS):
            at_copy(s, j).wait_recv()

        def piece(n):
            i = lax.rem(z + n, ZS)
            part = dot_nn(uu[i, 0], att_all[0, j])
            for row in range(1, XS):
                part = part + dot_nn(uu[i, row], att_all[row, j])
            return part.astype(BF16)

        def send(n, carry):
            wos[n, j] = piece(n)
            wo_copy(n, j).start()
            return carry

        lax.fori_loop(1, ZS, send, 0)
        wor[z, j] = piece(0)

    def stage(t, carry):
        @pl.when(t < HEADS)
        def _():
            relay(t)

        @pl.when(t == 1)
        def _():
            context()

        @pl.when(t >= 1)
        def _():
            head(t - 1)

        @pl.when(t == 1)
        def _():
            spread_columns()

        @pl.when(t == 3)
        def _():
            finish_columns()

        @pl.when(t >= 3)
        def _():
            project(t - 3)

        @pl.when(t >= 2)
        def _():
            chain_one(t - 2)

        @pl.when(t >= 3)
        def _():
            chain_two(t - 3)

        return carry

    lax.fori_loop(0, HEADS + 1, stage, 0)
    project(2)
    project(3)
    chain_one(3)
    chain_two(2)
    last(0)
    last(1)
    chain_two(3)
    last(2)
    last(3)

    def gather(j, carry):
        for n in range(1, ZS):
            wo_copy(n, j).wait_recv()
        total = wor[0, j].astype(F32)
        for n in range(1, ZS):
            total = total + wor[n, j].astype(F32)
        wo_o[:, cols(j, HDIM)] = total
        return carry

    lax.fori_loop(0, HEADS, gather, 0)

    def drain(j, carry):
        for lv in range(1, LV):
            kv_copy(lv, j).wait_send()
            gr_copy(lv, j).wait_send()
        for s in range(1, XS):
            at_copy(s, j).wait_send()
        for n in range(1, ZS):
            wo_copy(n, j).wait_send()
        return carry

    lax.fori_loop(0, HEADS, drain, 0)
    fc_copy(0).wait_send()
    uc_copy(0).wait_send()
    for s in range(1, XS):
        fy_copy(s).wait_send()
        fc_copy(s).wait_send()
        ua_copy(s).wait_send()
        uy_copy(s).wait_send()
        uc_copy(s).wait_send()


def hand_over(*refs):
    copies = [pltpu.make_async_copy(refs[i], refs[5 + i], refs[10].at[i]) for i in range(5)]
    for copy in copies:
        copy.start()
    for copy in copies:
        copy.wait()


def per_device(queries, keys, values, upstream, out_weight):
    tokens = jax.ShapeDtypeStruct((BLK, FEAT), BF16)
    shapes = (tokens, tokens, tokens, tokens, jax.ShapeDtypeStruct((HDIM, FEAT), F32))
    dma = pltpu.SemaphoreType.DMA
    vmem = pltpu.VMEM
    results = pl.pallas_call(
        kernel,
        out_shape=shapes,
        in_specs=[pl.BlockSpec(memory_space=pl.ANY)] * 5,
        out_specs=(pl.BlockSpec(memory_space=pltpu.VMEM),) * 5,
        scratch_shapes=[
            vmem((HEADS, 2, LV, BLK, HDIM), BF16),
            vmem((HEADS, BLK, HDIM), BF16),
            vmem((HP, BLK, FEAT), BF16),
            vmem((FEAT, D), BF16),
            vmem((XS, HDIM, BLK), BF16),
            vmem((HP, XS, HDIM, BLK), BF16),
            vmem((BLK, FEAT), F32),
            vmem((HEADS, BLK, HDIM), BF16),
            vmem((LV, BLK, BLK), F32),
            vmem((LV * BLK, BLK), BF16),
            vmem((XS, HEADS, BLK, HDIM), BF16),
            vmem((5, HEADS, 2, BLK, HDIM), F32),
            vmem((5, HEADS, 2, BLK, HDIM), BF16),
            vmem((5, HEADS, 2, BLK, HDIM), BF16),
            vmem((ZS, HEADS, HDIM, HDIM), BF16),
            vmem((ZS, HEADS, HDIM, HDIM), BF16),
            dma((14,)),
            dma((5, HEADS)), dma((5, HEADS)),
            dma((5, HEADS)), dma((5, HEADS)),
            dma((XS,)), dma((XS,)), dma((XS,)), dma((XS,)),
            dma((XS,)), dma((XS,)),
            dma((XS,)), dma((XS,)), dma((XS,)), dma((XS,)),
            dma((XS, HEADS)), dma((XS, HEADS)),
            dma((ZS, HEADS)), dma((ZS, HEADS)),
        ],
        compiler_params=pltpu.CompilerParams(
            collective_id=0, has_side_effects=True, vmem_limit_bytes=52 * 1024 * 1024
        ),
        cost_estimate=pl.CostEstimate(flops=5 * 10**9, bytes_accessed=10**7, transcendentals=2 * 10**6),
        name="log_sparse_attention",
    )(queries, keys, values, upstream, out_weight)
    return pl.pallas_call(
        hand_over,
        out_shape=shapes,
        in_specs=[pl.BlockSpec(memory_space=pltpu.VMEM)] * 5,
        out_specs=(pl.BlockSpec(memory_space=pl.ANY),) * 5,
        scratch_shapes=[dma((5,))],
        compiler_params=pltpu.CompilerParams(vmem_limit_bytes=4 * 1024 * 1024),
        name="hand_over",
    )(*results)


def solution(mesh):
    tiled = P("ctx", "head")
    return jax.shard_map(
        per_device,
        mesh=mesh,
        in_specs=(tiled, tiled, tiled, tiled, P("head", None)),
        out_specs=(tiled,) * 5,
        check_vma=False,
    )
```

```python
import math

import jax
import jax.numpy as jnp
from jax import lax
from jax.experimental import pallas as pl
from jax.experimental.pallas import tpu as pltpu
from jax.sharding import PartitionSpec as P

HDIM = 128
BLK = 256
DISTANCES = (0, 1, 2, 4, 8, 16)
LV = len(DISTANCES)
HEADS = 4
FEAT = HEADS * HDIM
D = 4096
CTX = 32
ZS = 8
XS = 4
UP = 4
DOWN = 3
GROUPS = 2
WIDE = FEAT // GROUPS
HP = 8
SCALING = 1.0 / math.sqrt(HDIM)
MESH = pl.DeviceIdType.MESH
BF16 = jnp.bfloat16
F32 = jnp.float32

KV_ROUTE = {1: (0, 1), 2: (1, 1), 3: (2, 2), 4: (0, 8), 5: (4, 8)}


def dot_nt(a, b):
    return lax.dot_general(a, b, (((1,), (1,)), ((), ())), preferred_element_type=F32)


def dot_nn(a, b):
    return lax.dot_general(a, b, (((1,), (0,)), ((), ())), preferred_element_type=F32)


def dot_tn(a, b):
    return lax.dot_general(a, b, (((0,), (0,)), ((), ())), preferred_element_type=F32)


def kernel(
    q_in, k_in, v_in, up_in, w_in,
    att_o, dq_o, dk_o, dv_o, wo_o,
    kv, held, qh, fu, wv, ust, uu, cg_acc, cgh, sc, nb, att_all, own, gs, gr, held_gr, part, wos, wor,
    loc, kv_s, kv_r, nk_s, nk_r, gr_s, gr_r, gn_s, gn_r, fy_s, fy_r, fc_s, fc_r, ua_s, ua_r, uy_s, uy_r, uc_s, uc_r,
    at_s, at_r, wo_s, wo_r,
):
    c = lax.axis_index("ctx")
    h = lax.axis_index("head")
    x = lax.div(c, ZS)
    z = lax.rem(c, ZS)
    core = lax.rem(h, 2)
    twin = h + 1 - 2 * core

    def at_ctx(shift):
        return (lax.rem(c + (shift + CTX), CTX), h)

    def at_z(shift):
        return (x * ZS + lax.rem(z + (shift + ZS), ZS), h)

    def at_head(shift):
        return (c, lax.rem(h + shift, HP))

    def cols(j, width):
        return pl.ds(pl.multiple_of(j * width, 128), width)

    def remote(src, dst, send, recv, device):
        return pltpu.make_async_remote_copy(
            src, dst, send, recv, device_id=device, device_id_type=MESH)

    def local_copy(kind, j):
        src = (k_in, v_in, q_in)[kind].at[:, j * HDIM : (j + 1) * HDIM]
        dst = qh.at[j] if kind == 2 else kv.at[j, kind, 0]
        return pltpu.make_async_copy(src, dst, loc.at[kind * HEADS + j])

    up_copy = pltpu.make_async_copy(up_in, fu.at[h], loc.at[12])
    w_copy = pltpu.make_async_copy(w_in, wv, loc.at[13])

    def kv_copy(lv, j, src=None):
        route, shift = KV_ROUTE[lv]
        return remote(
            kv.at[j, :, route if src is None else src], kv.at[j, :, lv],
            kv_s.at[lv - 1, j], kv_r.at[lv - 1, j], at_z(1) if lv == 1 else at_ctx(shift))

    def gr_copy(lv, j):
        return remote(
            gs.at[lv - 1, j], gr.at[lv - 1, j], gr_s.at[lv - 1, j], gr_r.at[lv - 1, j],
            at_ctx(-KV_ROUTE[lv][1]))

    def nk_copy(j, src):
        return remote(kv.at[j, :, src], held.at[j], nk_s.at[j], nk_r.at[j], at_z(-2))

    def nk_relay(j):
        return remote(held.at[j], kv.at[j, :, 3], kv_s.at[2, j], kv_r.at[2, j], at_z(-2))

    def gn_copy(j):
        return remote(gs.at[2, j], held_gr.at[j - 2], gn_s.at[j - 2], gn_r.at[j - 2], at_z(2))

    def gn_relay(j):
        return remote(held_gr.at[j - 2], gr.at[2, j], gr_s.at[2, j], gr_r.at[2, j], at_z(2))

    def from_y(s):
        return lax.rem(h + (HP - 2 * s), HP)

    def fy_copy(s):
        return remote(up_in, fu.at[h], fy_s.at[s], fy_r.at[s], at_head(2 * s))

    def fc_copy(s):
        slot = from_y(s)
        return remote(up_in if s == 0 else fu.at[slot], fu.at[slot], fc_s.at[s], fc_r.at[s], (c, twin))

    def ua_copy(s):
        return remote(ust.at[s], uu.at[h, x], ua_s.at[s], ua_r.at[s], at_ctx(s * ZS))

    def uy_copy(s):
        return remote(uu.at[h], uu.at[h], uy_s.at[s], uy_r.at[s], at_head(2 * s))

    def uc_copy(s):
        slot = from_y(s)
        return remote(uu.at[slot], uu.at[slot], uc_s.at[s], uc_r.at[s], (c, twin))

    def at_copy(s, j):
        piece = att_all.at[x, lax.div(j, 2), :, cols(lax.rem(j, 2), HDIM)]
        return remote(piece, piece, at_s.at[s, j], at_r.at[s, j], at_ctx(s * ZS))

    def wo_copy(g, way, k):
        return remote(
            wos.at[g, way, k], wor.at[g, way, k], wo_s.at[g, way, k], wo_r.at[g, way, k],
            at_z(1 - 2 * way))

    for j in range(HEADS):
        local_copy(0, j).start()
        local_copy(1, j).start()
    up_copy.start()
    for j in range(HEADS):
        local_copy(2, j).start()
    w_copy.start()

    barrier = pltpu.get_barrier_semaphore()
    peers = [at_ctx(shift) for shift in (1, -1, 2, -2, 8, 16, 24)]
    peers += [at_head(s) for s in (2, 4, 6)] + [(c, twin)]
    peers += [at_z(s) for s in (1, -1, 2, -2)]
    for peer in peers:
        pl.semaphore_signal(barrier, inc=1, device_id=peer, device_id_type=MESH)
    pl.semaphore_wait(barrier, len(peers))

    for j in range(HEADS):
        local_copy(0, j).wait()
        local_copy(1, j).wait()
        if j < 2:
            @pl.when(z < ZS - 1)
            def _():
                kv_copy(1, j).start()

            @pl.when(z < ZS // 2)
            def _():
                nk_copy(j, 0).start()

        kv_copy(4, j).start()
        if j == 0:
            fc_copy(0).start()
            for s in range(1, XS):
                fy_copy(s).start()

    def relay_near(j):
        kv_copy(4, j).wait_recv()
        kv_copy(5, j).start()

        @pl.when(z == ZS - 1)
        def _():
            kv_copy(1, j, 4).start()

        if j < 2:
            @pl.when(z >= ZS // 2)
            def _():
                nk_copy(j, 4).start()

        kv_copy(1, j).wait_recv()
        kv_copy(2, j).start()

        if j < 2:
            @pl.when(z < ZS - 1)
            def _():
                kv_copy(1, j + 2).start()

    def relay_down(j):
        nk_copy(j, 0).wait_recv()
        nk_relay(j).start()

    def relay_up(j):
        kv_copy(2, j).wait_recv()
        kv_copy(3, j).start()

    def pass_upstream():
        for s in range(1, XS):
            fy_copy(s).wait_recv()
            fc_copy(s).start()

    def exchange_columns():
        for s in range(XS):
            fc_copy(s).wait_recv()
        up_copy.wait()
        for s in range(XS):
            target = lax.rem(x + s, XS)
            tile = fu[2 * target + lax.div(h, 4), :, cols(lax.rem(h, 4), HDIM)].T
            if s == 0:
                uu[h, x] = tile
            else:
                ust[s] = tile
                ua_copy(s).start()

    def context():
        w_copy.wait()
        cg_acc[...] = dot_nt(fu[0], wv[:, 0:FEAT])

        def add_tile(tile, carry):
            cg_acc[...] += dot_nt(fu[tile], wv[:, cols(tile, FEAT)])
            return carry

        lax.fori_loop(1, HP, add_tile, 0)
        for j in range(HEADS):
            cgh[j] = cg_acc[:, j * HDIM : (j + 1) * HDIM].astype(BF16)
            local_copy(2, j).wait()

    def spread_columns():
        for s in range(1, XS):
            ua_copy(s).wait_recv()
        uc_copy(0).start()
        for s in range(1, XS):
            uy_copy(s).start()

    def finish_columns():
        for s in range(1, XS):
            uy_copy(s).wait_recv()
            uc_copy(s).start()
        for s in range(XS):
            uc_copy(s).wait_recv()

    def head(j):
        @pl.when(j < 2)
        def _():
            kv_copy(2, j).wait_recv()

        kv_copy(3, j).wait_recv()
        kv_copy(5, j).wait_recv()
        q = qh[j]
        cg = cgh[j]
        row_max = None
        for lv in range(LV):
            s = dot_nt(kv[j, 0, lv], q) * SCALING
            if lv == 0:
                key_id = lax.broadcasted_iota(jnp.int32, (BLK, BLK), 0)
                query_id = lax.broadcasted_iota(jnp.int32, (BLK, BLK), 1)
                s = jnp.where(key_id <= query_id, s, -1e30)
            else:
                s = s + jnp.where(c >= DISTANCES[lv], 0.0, -1e30).astype(F32)
            sc[lv] = s
            top = jnp.max(s, axis=0, keepdims=True)
            row_max = top if row_max is None else jnp.maximum(row_max, top)
        totals = jnp.zeros((1, BLK), F32)
        for lv in range(LV):
            w = jnp.exp(sc[lv] - row_max)
            sc[lv] = w
            totals = totals + jnp.sum(w, axis=0, keepdims=True)
            nb[lv * BLK : (lv + 1) * BLK, :] = w.astype(BF16)
        inverse = 1.0 / totals
        mixed = dot_tn(kv[j, 1].reshape(LV * BLK, HDIM), nb[...])
        att_t = (mixed * inverse).astype(BF16).astype(F32)
        att = att_t.T.astype(BF16)
        att_o[:, cols(j, HDIM)] = att
        att_all[x, lax.div(j, 2), :, cols(lax.rem(j, 2), HDIM)] = att
        for s in range(1, XS):
            at_copy(s, j).start()
        row_dots = jnp.sum(cg.astype(F32).T * att_t, axis=0, keepdims=True)
        for lv in range(LV):
            normed = sc[lv] * inverse
            prob_grad = dot_nt(kv[j, 1, lv], cg)
            ds = (normed * (prob_grad - row_dots)).astype(BF16)
            nb[lv * BLK : (lv + 1) * BLK, :] = ds
            dv = dot_nn(normed.astype(BF16), cg)
            dk = dot_nn(ds, q) * SCALING
            if lv in (3, 5):
                gs[lv - 1, j, 0] = dk.astype(BF16)
                gs[lv - 1, j, 1] = dv.astype(BF16)
                if lv == 5:
                    gr_copy(lv, j).start()
                else:
                    @pl.when(j < 2)
                    def _():
                        gr_copy(3, j).start()

                    @pl.when(j >= 2)
                    def _():
                        gn_copy(j).start()
            else:
                own[lv, j, 0] = dk
                own[lv, j, 1] = dv
                if lv == 2:
                    @pl.when(j >= 2)
                    def _():
                        gs[1, j, 0] = dk.astype(BF16)
                        gs[1, j, 1] = dv.astype(BF16)
                        gr_copy(2, j).start()
        dq_t = dot_tn(kv[j, 0].reshape(LV * BLK, HDIM), nb[...]) * SCALING
        dq_o[:, cols(j, HDIM)] = dq_t.T.astype(BF16)

    def pass_on(src, dst, j):
        gr_copy(src, j).wait_recv()
        gs[dst - 1, j] = (own[dst, j] + gr[src - 1, j].astype(F32)).astype(BF16)
        gr_copy(dst, j).start()

    def chain_one(j):
        pass_on(3, 2, j)

    def chain_two(j):
        pass_on(2, 1, j)

    def send_up(j):
        gn_copy(j).wait_recv()
        gn_relay(j).start()

    upper = (z >= ZS // 2).astype(F32)

    def eight(j):
        if j < 2:
            pass_on(5, 4, j)
        else:
            gr_copy(5, j).wait_recv()
            gr_copy(3, j).wait_recv()
            total = own[4, j] + gr[4, j].astype(F32) + upper * gr[2, j].astype(F32)
            gs[3, j] = total.astype(BF16)
            gr_copy(4, j).start()

    def last(j):
        gr_copy(1, j).wait_recv()
        gr_copy(4, j).wait_recv()
        total = own[0, j] + gr[0, j].astype(F32) + gr[3, j].astype(F32)
        if j >= 2:
            total = total + (1.0 - upper) * gr[2, j].astype(F32)
        dk_o[:, cols(j, HDIM)] = total[0].astype(BF16)
        dv_o[:, cols(j, HDIM)] = total[1].astype(BF16)

    def project(g):
        for j in (2 * g, 2 * g + 1):
            for s in range(1, XS):
                at_copy(s, j).wait_recv()

        def pieces(n, carry):
            rows = pl.ds(n * 4, 4)
            total = dot_nn(uu[rows, 0].reshape(4 * HDIM, BLK), att_all[0, g])
            for row in range(1, XS):
                total = total + dot_nn(uu[rows, row].reshape(4 * HDIM, BLK), att_all[row, g])
            part[g, rows] = total.reshape(4, HDIM, WIDE)
            return carry

        lax.fori_loop(0, ZS // 4, pieces, 0)
        for way, steps in ((0, UP), (1, DOWN)):
            wos[g, way, 0] = part[g, target_of(way, steps)].astype(BF16)
            wo_copy(g, way, 0).start()

    def target_of(way, left):
        return lax.rem(z + (left if way == 0 else ZS - left), ZS)

    def ring(g, k):
        for way, steps in ((0, UP), (1, DOWN)):
            if k > steps:
                continue
            wo_copy(g, way, k - 1).wait_recv()
            if k < steps:
                total = wor[g, way, k - 1].astype(F32) + part[g, target_of(way, steps - k)]
                wos[g, way, k] = total.astype(BF16)
                wo_copy(g, way, k).start()
            elif way == 1:
                part[g, z] = part[g, z] + wor[g, way, k - 1].astype(F32)
            else:
                wo_o[:, g * WIDE : (g + 1) * WIDE] = part[g, z] + wor[g, way, k - 1].astype(F32)

    relay_near(0)
    relay_down(0)
    relay_near(1)
    pass_upstream()
    relay_down(1)
    relay_near(2)
    exchange_columns()
    relay_near(3)
    context()
    relay_up(2)

    def stage(t, carry):
        @pl.when(t == 1)
        def _():
            relay_up(3)

        @pl.when(t == 2)
        def _():
            spread_columns()

        @pl.when(t == 3)
        def _():
            chain_one(0)

        head(t)
        return carry

    lax.fori_loop(0, HEADS, stage, 0)
    chain_one(1)
    send_up(2)
    finish_columns()
    chain_two(2)
    project(0)
    project(1)
    eight(1)
    chain_two(0)
    ring(0, 1)
    ring(1, 1)
    send_up(3)
    eight(2)
    chain_two(1)
    ring(0, 2)
    ring(1, 2)
    eight(0)
    last(1)
    chain_two(3)
    eight(3)
    ring(0, 3)
    ring(1, 3)
    last(0)
    last(2)
    ring(0, 4)
    last(3)
    ring(1, 4)

    def drain(j, carry):
        for lv in range(1, LV):
            kv_copy(lv, j).wait_send()
            gr_copy(lv, j).wait_send()
        for s in range(1, XS):
            at_copy(s, j).wait_send()
        return carry

    lax.fori_loop(0, HEADS, drain, 0)
    for j in (0, 1):
        nk_copy(j, 0).wait_send()
        gn_copy(j + 2).wait_send()
    for g in range(GROUPS):
        for way, steps in ((0, UP), (1, DOWN)):
            for k in range(steps):
                wo_copy(g, way, k).wait_send()
    fc_copy(0).wait_send()
    uc_copy(0).wait_send()
    for s in range(1, XS):
        fy_copy(s).wait_send()
        fc_copy(s).wait_send()
        ua_copy(s).wait_send()
        uy_copy(s).wait_send()
        uc_copy(s).wait_send()


def hand_over(*refs):
    copies = [pltpu.make_async_copy(refs[i], refs[5 + i], refs[10].at[i]) for i in range(5)]
    for copy in copies:
        copy.start()
    for copy in copies:
        copy.wait()


def per_device(queries, keys, values, upstream, out_weight):
    tokens = jax.ShapeDtypeStruct((BLK, FEAT), BF16)
    shapes = (tokens, tokens, tokens, tokens, jax.ShapeDtypeStruct((HDIM, FEAT), F32))
    dma = pltpu.SemaphoreType.DMA
    vmem = pltpu.VMEM
    results = pl.pallas_call(
        kernel,
        out_shape=shapes,
        in_specs=[pl.BlockSpec(memory_space=pl.ANY)] * 5,
        out_specs=(pl.BlockSpec(memory_space=pltpu.VMEM),) * 5,
        scratch_shapes=[
            vmem((HEADS, 2, LV, BLK, HDIM), BF16),
            vmem((2, 2, BLK, HDIM), BF16),
            vmem((HEADS, BLK, HDIM), BF16),
            vmem((HP, BLK, FEAT), BF16),
            vmem((FEAT, D), BF16),
            vmem((XS, HDIM, BLK), BF16),
            vmem((HP, XS, HDIM, BLK), BF16),
            vmem((BLK, FEAT), F32),
            vmem((HEADS, BLK, HDIM), BF16),
            vmem((LV, BLK, BLK), F32),
            vmem((LV * BLK, BLK), BF16),
            vmem((XS, GROUPS, BLK, WIDE), BF16),
            vmem((5, HEADS, 2, BLK, HDIM), F32),
            vmem((5, HEADS, 2, BLK, HDIM), BF16),
            vmem((5, HEADS, 2, BLK, HDIM), BF16),
            vmem((2, 2, BLK, HDIM), BF16),
            vmem((GROUPS, ZS, HDIM, WIDE), F32),
            vmem((GROUPS, 2, UP, HDIM, WIDE), BF16),
            vmem((GROUPS, 2, UP, HDIM, WIDE), BF16),
            dma((14,)),
            dma((5, HEADS)), dma((5, HEADS)),
            dma((2,)), dma((2,)),
            dma((5, HEADS)), dma((5, HEADS)),
            dma((2,)), dma((2,)),
            dma((XS,)), dma((XS,)), dma((XS,)), dma((XS,)),
            dma((XS,)), dma((XS,)),
            dma((XS,)), dma((XS,)), dma((XS,)), dma((XS,)),
            dma((XS, HEADS)), dma((XS, HEADS)),
            dma((GROUPS, 2, UP)), dma((GROUPS, 2, UP)),
        ],
        compiler_params=pltpu.CompilerParams(
            collective_id=0, has_side_effects=True, vmem_limit_bytes=52 * 1024 * 1024
        ),
        cost_estimate=pl.CostEstimate(flops=5 * 10**9, bytes_accessed=10**7, transcendentals=2 * 10**6),
        name="log_sparse_attention",
    )(queries, keys, values, upstream, out_weight)
    return pl.pallas_call(
        hand_over,
        out_shape=shapes,
        in_specs=[pl.BlockSpec(memory_space=pltpu.VMEM)] * 5,
        out_specs=(pl.BlockSpec(memory_space=pl.ANY),) * 5,
        scratch_shapes=[dma((5,))],
        compiler_params=pltpu.CompilerParams(vmem_limit_bytes=4 * 1024 * 1024),
        name="hand_over",
    )(*results)


def solution(mesh):
    tiled = P("ctx", "head")
    return jax.shard_map(
        per_device,
        mesh=mesh,
        in_specs=(tiled, tiled, tiled, tiled, P("head", None)),
        out_specs=(tiled,) * 5,
        check_vma=False,
    )
```

```python
import math

import jax
import jax.numpy as jnp
from jax import lax
from jax.experimental import pallas as pl
from jax.experimental.pallas import tpu as pltpu
from jax.sharding import PartitionSpec as P

HDIM = 128
BLK = 256
DISTANCES = (0, 1, 2, 4, 8, 16)
LV = len(DISTANCES)
HEADS = 4
FEAT = HEADS * HDIM
D = 4096
CTX = 32
ZS = 8
XS = 4
UP = 4
DOWN = 3
GROUPS = 2
WIDE = FEAT // GROUPS
HP = 8
SCALING = 1.0 / math.sqrt(HDIM)
MESH = pl.DeviceIdType.MESH
BF16 = jnp.bfloat16
F32 = jnp.float32

KV_ROUTE = {1: (0, 1), 2: (1, 1), 3: (2, 2), 4: (0, 8), 5: (4, 8)}


def dot_nt(a, b):
    return lax.dot_general(a, b, (((1,), (1,)), ((), ())), preferred_element_type=F32)


def dot_nn(a, b):
    return lax.dot_general(a, b, (((1,), (0,)), ((), ())), preferred_element_type=F32)


def dot_tn(a, b):
    return lax.dot_general(a, b, (((0,), (0,)), ((), ())), preferred_element_type=F32)


def kernel(
    q_in, k_in, v_in, up_in, w_in,
    att_o, dq_o, dk_o, dv_o, wo_o,
    kv, held, qh, fu, wv, ust, uu, cg_acc, cgh, sc, nb, att_all, own, gs, gr, held_gr, part, wos, wor,
    loc, kv_s, kv_r, nk_s, nk_r, gr_s, gr_r, gn_s, gn_r, fy_s, fy_r, fc_s, fc_r, ua_s, ua_r, uy_s, uy_r, uc_s, uc_r,
    at_s, at_r, wo_s, wo_r,
):
    c = lax.axis_index("ctx")
    h = lax.axis_index("head")
    x = lax.div(c, ZS)
    z = lax.rem(c, ZS)
    core = lax.rem(h, 2)
    twin = h + 1 - 2 * core

    def at_ctx(shift):
        return (lax.rem(c + (shift + CTX), CTX), h)

    def at_z(shift):
        return (x * ZS + lax.rem(z + (shift + ZS), ZS), h)

    def at_head(shift):
        return (c, lax.rem(h + shift, HP))

    def cols(j, width):
        return pl.ds(pl.multiple_of(j * width, 128), width)

    def remote(src, dst, send, recv, device):
        return pltpu.make_async_remote_copy(
            src, dst, send, recv, device_id=device, device_id_type=MESH)

    def local_copy(kind, j):
        src = (k_in, v_in, q_in)[kind].at[:, j * HDIM : (j + 1) * HDIM]
        dst = qh.at[j] if kind == 2 else kv.at[j, kind, 0]
        return pltpu.make_async_copy(src, dst, loc.at[kind * HEADS + j])

    up_copy = pltpu.make_async_copy(up_in, fu.at[h], loc.at[12])
    w_copy = pltpu.make_async_copy(w_in, wv, loc.at[13])

    def kv_copy(lv, j, src=None):
        route, shift = KV_ROUTE[lv]
        return remote(
            kv.at[j, :, route if src is None else src], kv.at[j, :, lv],
            kv_s.at[lv - 1, j], kv_r.at[lv - 1, j], at_z(1) if lv == 1 else at_ctx(shift))

    def gr_copy(lv, j):
        return remote(
            gs.at[lv - 1, j], gr.at[lv - 1, j], gr_s.at[lv - 1, j], gr_r.at[lv - 1, j],
            at_ctx(-KV_ROUTE[lv][1]))

    def nk_copy(j, src):
        return remote(kv.at[j, :, src], held.at[j], nk_s.at[j], nk_r.at[j], at_z(-2))

    def nk_relay(j):
        return remote(held.at[j], kv.at[j, :, 3], kv_s.at[2, j], kv_r.at[2, j], at_z(-2))

    def gn_copy(j):
        return remote(gs.at[2, j], held_gr.at[j - 2], gn_s.at[j - 2], gn_r.at[j - 2], at_z(2))

    def gn_relay(j):
        return remote(held_gr.at[j - 2], gr.at[2, j], gr_s.at[2, j], gr_r.at[2, j], at_z(2))

    def from_y(s):
        return lax.rem(h + (HP - 2 * s), HP)

    def fy_copy(s):
        return remote(up_in, fu.at[h], fy_s.at[s], fy_r.at[s], at_head(2 * s))

    def fc_copy(s):
        slot = from_y(s)
        return remote(up_in if s == 0 else fu.at[slot], fu.at[slot], fc_s.at[s], fc_r.at[s], (c, twin))

    def ua_copy(s):
        return remote(ust.at[s], uu.at[h, x], ua_s.at[s], ua_r.at[s], at_ctx(s * ZS))

    def uy_copy(s):
        return remote(uu.at[h], uu.at[h], uy_s.at[s], uy_r.at[s], at_head(2 * s))

    def uc_copy(s):
        slot = from_y(s)
        return remote(uu.at[slot], uu.at[slot], uc_s.at[s], uc_r.at[s], (c, twin))

    def at_copy(s, j):
        piece = att_all.at[x, lax.div(j, 2), :, cols(lax.rem(j, 2), HDIM)]
        return remote(piece, piece, at_s.at[s, j], at_r.at[s, j], at_ctx(s * ZS))

    def wo_copy(g, way, k):
        return remote(
            wos.at[g, way, k], wor.at[g, way, k], wo_s.at[g, way, k], wo_r.at[g, way, k],
            at_z(1 - 2 * way))

    for j in range(HEADS):
        local_copy(0, j).start()
        local_copy(1, j).start()
    up_copy.start()
    for j in range(HEADS):
        local_copy(2, j).start()
    w_copy.start()

    barrier = pltpu.get_barrier_semaphore()
    peers = [at_ctx(shift) for shift in (1, -1, 2, -2, 8, 16, 24)]
    peers += [at_head(s) for s in (2, 4, 6)] + [(c, twin)]
    peers += [at_z(s) for s in (1, -1, 2, -2)]
    for peer in peers:
        pl.semaphore_signal(barrier, inc=1, device_id=peer, device_id_type=MESH)
    pl.semaphore_wait(barrier, len(peers))

    for j in range(HEADS):
        local_copy(0, j).wait()
        local_copy(1, j).wait()
        if j < 2:
            @pl.when(z < ZS - 1)
            def _():
                kv_copy(1, j).start()

            @pl.when(z < ZS // 2)
            def _():
                nk_copy(j, 0).start()

        kv_copy(4, j).start()
        if j == 0:
            fc_copy(0).start()
            for s in range(1, XS):
                fy_copy(s).start()

    def relay_near(j):
        kv_copy(4, j).wait_recv()
        kv_copy(5, j).start()

        @pl.when(z == ZS - 1)
        def _():
            kv_copy(1, j, 4).start()

        if j < 2:
            @pl.when(z >= ZS // 2)
            def _():
                nk_copy(j, 4).start()

        kv_copy(1, j).wait_recv()
        kv_copy(2, j).start()

        if j < 2:
            @pl.when(z < ZS - 1)
            def _():
                kv_copy(1, j + 2).start()

    def relay_down(j):
        nk_copy(j, 0).wait_recv()
        nk_relay(j).start()

    def relay_up(j):
        kv_copy(2, j).wait_recv()
        kv_copy(3, j).start()

    def pass_upstream():
        for s in range(1, XS):
            fy_copy(s).wait_recv()
            fc_copy(s).start()

    def exchange_columns():
        for s in range(XS):
            fc_copy(s).wait_recv()
        up_copy.wait()
        for s in range(XS):
            target = lax.rem(x + s, XS)
            tile = fu[2 * target + lax.div(h, 4), :, cols(lax.rem(h, 4), HDIM)].T
            if s == 0:
                uu[h, x] = tile
            else:
                ust[s] = tile
                ua_copy(s).start()

    def context():
        w_copy.wait()
        cg_acc[...] = dot_nt(fu[0], wv[:, 0:FEAT])

        def add_tile(tile, carry):
            cg_acc[...] += dot_nt(fu[tile], wv[:, cols(tile, FEAT)])
            return carry

        lax.fori_loop(1, HP, add_tile, 0)
        for j in range(HEADS):
            cgh[j] = cg_acc[:, j * HDIM : (j + 1) * HDIM].astype(BF16)
            local_copy(2, j).wait()

    def spread_columns():
        for s in range(1, XS):
            ua_copy(s).wait_recv()
        uc_copy(0).start()
        for s in range(1, XS):
            uy_copy(s).start()

    def finish_columns():
        for s in range(1, XS):
            uy_copy(s).wait_recv()
            uc_copy(s).start()
        for s in range(XS):
            uc_copy(s).wait_recv()

    def head(j):
        @pl.when(j < 2)
        def _():
            kv_copy(2, j).wait_recv()

        kv_copy(3, j).wait_recv()
        kv_copy(5, j).wait_recv()
        q = qh[j]
        cg = cgh[j]
        row_max = None
        for lv in range(LV):
            s = dot_nt(kv[j, 0, lv], q) * SCALING
            if lv == 0:
                key_id = lax.broadcasted_iota(jnp.int32, (BLK, BLK), 0)
                query_id = lax.broadcasted_iota(jnp.int32, (BLK, BLK), 1)
                s = jnp.where(key_id <= query_id, s, -1e30)
            else:
                s = s + jnp.where(c >= DISTANCES[lv], 0.0, -1e30).astype(F32)
            sc[lv] = s
            top = jnp.max(s, axis=0, keepdims=True)
            row_max = top if row_max is None else jnp.maximum(row_max, top)
        totals = jnp.zeros((1, BLK), F32)
        for lv in range(LV):
            w = jnp.exp(sc[lv] - row_max)
            sc[lv] = w
            totals = totals + jnp.sum(w, axis=0, keepdims=True)
            nb[lv * BLK : (lv + 1) * BLK, :] = w.astype(BF16)
        inverse = 1.0 / totals
        mixed = dot_tn(kv[j, 1].reshape(LV * BLK, HDIM), nb[...])
        att_t = (mixed * inverse).astype(BF16).astype(F32)
        att = att_t.T.astype(BF16)
        att_o[:, cols(j, HDIM)] = att
        att_all[x, lax.div(j, 2), :, cols(lax.rem(j, 2), HDIM)] = att
        for s in range(1, XS):
            at_copy(s, j).start()
        row_dots = jnp.sum(cg.astype(F32).T * att_t, axis=0, keepdims=True)
        for lv in (3, 5, 2, 4, 1, 0):
            normed = sc[lv] * inverse
            prob_grad = dot_nt(kv[j, 1, lv], cg)
            ds = (normed * (prob_grad - row_dots)).astype(BF16)
            nb[lv * BLK : (lv + 1) * BLK, :] = ds
            dv = dot_nn(normed.astype(BF16), cg)
            dk = dot_nn(ds, q) * SCALING
            if lv in (3, 5):
                gs[lv - 1, j, 0] = dk.astype(BF16)
                gs[lv - 1, j, 1] = dv.astype(BF16)
                if lv == 5:
                    gr_copy(lv, j).start()
                else:
                    @pl.when(j < 2)
                    def _():
                        gr_copy(3, j).start()

                    @pl.when(j >= 2)
                    def _():
                        gn_copy(j).start()
            else:
                own[lv, j, 0] = dk
                own[lv, j, 1] = dv
                if lv == 2:
                    @pl.when(j >= 2)
                    def _():
                        gs[1, j, 0] = dk.astype(BF16)
                        gs[1, j, 1] = dv.astype(BF16)
                        gr_copy(2, j).start()
        dq_t = dot_tn(kv[j, 0].reshape(LV * BLK, HDIM), nb[...]) * SCALING
        dq_o[:, cols(j, HDIM)] = dq_t.T.astype(BF16)

    def pass_on(src, dst, j):
        gr_copy(src, j).wait_recv()
        gs[dst - 1, j] = (own[dst, j] + gr[src - 1, j].astype(F32)).astype(BF16)
        gr_copy(dst, j).start()

    def chain_one(j):
        pass_on(3, 2, j)

    def chain_two(j):
        pass_on(2, 1, j)

    def send_up(j):
        gn_copy(j).wait_recv()
        gn_relay(j).start()

    upper = (z >= ZS // 2).astype(F32)

    def eight(j):
        if j < 2:
            pass_on(5, 4, j)
        else:
            gr_copy(5, j).wait_recv()
            gr_copy(3, j).wait_recv()
            total = own[4, j] + gr[4, j].astype(F32) + upper * gr[2, j].astype(F32)
            gs[3, j] = total.astype(BF16)
            gr_copy(4, j).start()

    def last(j):
        gr_copy(1, j).wait_recv()
        gr_copy(4, j).wait_recv()
        total = own[0, j] + gr[0, j].astype(F32) + gr[3, j].astype(F32)
        if j >= 2:
            total = total + (1.0 - upper) * gr[2, j].astype(F32)
        dk_o[:, cols(j, HDIM)] = total[0].astype(BF16)
        dv_o[:, cols(j, HDIM)] = total[1].astype(BF16)

    def project(g):
        for j in (2 * g, 2 * g + 1):
            for s in range(1, XS):
                at_copy(s, j).wait_recv()

        def pieces(n, carry):
            rows = pl.ds(n * 4, 4)
            total = dot_nn(uu[rows, 0].reshape(4 * HDIM, BLK), att_all[0, g])
            for row in range(1, XS):
                total = total + dot_nn(uu[rows, row].reshape(4 * HDIM, BLK), att_all[row, g])
            part[g, rows] = total.reshape(4, HDIM, WIDE)
            return carry

        lax.fori_loop(0, ZS // 4, pieces, 0)
        for way, steps in ((0, UP), (1, DOWN)):
            wos[g, way, 0] = part[g, target_of(way, steps)].astype(BF16)
            wo_copy(g, way, 0).start()

    def target_of(way, left):
        return lax.rem(z + (left if way == 0 else ZS - left), ZS)

    def ring(g, k):
        for way, steps in ((0, UP), (1, DOWN)):
            if k > steps:
                continue
            wo_copy(g, way, k - 1).wait_recv()
            if k < steps:
                total = wor[g, way, k - 1].astype(F32) + part[g, target_of(way, steps - k)]
                wos[g, way, k] = total.astype(BF16)
                wo_copy(g, way, k).start()
            elif way == 1:
                part[g, z] = part[g, z] + wor[g, way, k - 1].astype(F32)
            else:
                wo_o[:, g * WIDE : (g + 1) * WIDE] = part[g, z] + wor[g, way, k - 1].astype(F32)

    relay_near(0)
    relay_down(0)
    relay_near(1)
    pass_upstream()
    relay_down(1)
    relay_near(2)
    exchange_columns()
    relay_near(3)
    context()
    relay_up(2)

    def stage(t, carry):
        @pl.when(t == 1)
        def _():
            relay_up(3)

        @pl.when(t == 2)
        def _():
            spread_columns()

        @pl.when(t == 3)
        def _():
            chain_one(0)

        head(t)
        return carry

    lax.fori_loop(0, HEADS, stage, 0)
    chain_one(1)
    send_up(2)
    finish_columns()
    chain_two(2)
    project(0)
    project(1)
    eight(1)
    chain_two(0)
    ring(0, 1)
    ring(1, 1)
    send_up(3)
    eight(2)
    chain_two(1)
    ring(0, 2)
    ring(1, 2)
    eight(0)
    last(1)
    chain_two(3)
    eight(3)
    ring(0, 3)
    ring(1, 3)
    last(0)
    last(2)
    ring(0, 4)
    last(3)
    ring(1, 4)

    def drain(j, carry):
        for lv in range(1, LV):
            kv_copy(lv, j).wait_send()
            gr_copy(lv, j).wait_send()
        for s in range(1, XS):
            at_copy(s, j).wait_send()
        return carry

    lax.fori_loop(0, HEADS, drain, 0)
    for j in (0, 1):
        nk_copy(j, 0).wait_send()
        gn_copy(j + 2).wait_send()
    for g in range(GROUPS):
        for way, steps in ((0, UP), (1, DOWN)):
            for k in range(steps):
                wo_copy(g, way, k).wait_send()
    fc_copy(0).wait_send()
    uc_copy(0).wait_send()
    for s in range(1, XS):
        fy_copy(s).wait_send()
        fc_copy(s).wait_send()
        ua_copy(s).wait_send()
        uy_copy(s).wait_send()
        uc_copy(s).wait_send()


def hand_over(*refs):
    copies = [pltpu.make_async_copy(refs[i], refs[5 + i], refs[10].at[i]) for i in range(5)]
    for copy in copies:
        copy.start()
    for copy in copies:
        copy.wait()


def per_device(queries, keys, values, upstream, out_weight):
    tokens = jax.ShapeDtypeStruct((BLK, FEAT), BF16)
    shapes = (tokens, tokens, tokens, tokens, jax.ShapeDtypeStruct((HDIM, FEAT), F32))
    dma = pltpu.SemaphoreType.DMA
    vmem = pltpu.VMEM
    results = pl.pallas_call(
        kernel,
        out_shape=shapes,
        in_specs=[pl.BlockSpec(memory_space=pl.ANY)] * 5,
        out_specs=(pl.BlockSpec(memory_space=pltpu.VMEM),) * 5,
        scratch_shapes=[
            vmem((HEADS, 2, LV, BLK, HDIM), BF16),
            vmem((2, 2, BLK, HDIM), BF16),
            vmem((HEADS, BLK, HDIM), BF16),
            vmem((HP, BLK, FEAT), BF16),
            vmem((FEAT, D), BF16),
            vmem((XS, HDIM, BLK), BF16),
            vmem((HP, XS, HDIM, BLK), BF16),
            vmem((BLK, FEAT), F32),
            vmem((HEADS, BLK, HDIM), BF16),
            vmem((LV, BLK, BLK), F32),
            vmem((LV * BLK, BLK), BF16),
            vmem((XS, GROUPS, BLK, WIDE), BF16),
            vmem((5, HEADS, 2, BLK, HDIM), F32),
            vmem((5, HEADS, 2, BLK, HDIM), BF16),
            vmem((5, HEADS, 2, BLK, HDIM), BF16),
            vmem((2, 2, BLK, HDIM), BF16),
            vmem((GROUPS, ZS, HDIM, WIDE), F32),
            vmem((GROUPS, 2, UP, HDIM, WIDE), BF16),
            vmem((GROUPS, 2, UP, HDIM, WIDE), BF16),
            dma((14,)),
            dma((5, HEADS)), dma((5, HEADS)),
            dma((2,)), dma((2,)),
            dma((5, HEADS)), dma((5, HEADS)),
            dma((2,)), dma((2,)),
            dma((XS,)), dma((XS,)), dma((XS,)), dma((XS,)),
            dma((XS,)), dma((XS,)),
            dma((XS,)), dma((XS,)), dma((XS,)), dma((XS,)),
            dma((XS, HEADS)), dma((XS, HEADS)),
            dma((GROUPS, 2, UP)), dma((GROUPS, 2, UP)),
        ],
        compiler_params=pltpu.CompilerParams(
            collective_id=0, has_side_effects=True, vmem_limit_bytes=52 * 1024 * 1024 + 512 * 1024
        ),
        cost_estimate=pl.CostEstimate(flops=5 * 10**9, bytes_accessed=10**7, transcendentals=2 * 10**6),
        name="log_sparse_attention",
    )(queries, keys, values, upstream, out_weight)
    return pl.pallas_call(
        hand_over,
        out_shape=shapes,
        in_specs=[pl.BlockSpec(memory_space=pltpu.VMEM)] * 5,
        out_specs=(pl.BlockSpec(memory_space=pl.ANY),) * 5,
        scratch_shapes=[dma((5,))],
        compiler_params=pltpu.CompilerParams(vmem_limit_bytes=4 * 1024 * 1024),
        name="hand_over",
    )(*results)


def solution(mesh):
    tiled = P("ctx", "head")
    return jax.shard_map(
        per_device,
        mesh=mesh,
        in_specs=(tiled, tiled, tiled, tiled, P("head", None)),
        out_specs=(tiled,) * 5,
        check_vma=False,
    )
```

```python
import math

import jax
import jax.numpy as jnp
from jax import lax
from jax.experimental import pallas as pl
from jax.experimental.pallas import tpu as pltpu
from jax.sharding import PartitionSpec as P

HDIM = 128
BLK = 256
DISTANCES = (0, 1, 2, 4, 8, 16)
LV = len(DISTANCES)
HEADS = 4
FEAT = HEADS * HDIM
D = 4096
CTX = 32
ZS = 8
XS = 4
UP = 4
DOWN = 3
RISE = 2
GROUPS = 2
WIDE = FEAT // GROUPS
HP = 8
SCALING = 1.0 / math.sqrt(HDIM)
MESH = pl.DeviceIdType.MESH
BF16 = jnp.bfloat16
F32 = jnp.float32

KV_ROUTE = {1: (0, 1), 2: (1, 1), 3: (2, 2), 4: (0, 8), 5: (4, 8)}


def dot_nt(a, b):
    return lax.dot_general(a, b, (((1,), (1,)), ((), ())), preferred_element_type=F32)


def dot_nn(a, b):
    return lax.dot_general(a, b, (((1,), (0,)), ((), ())), preferred_element_type=F32)


def dot_tn(a, b):
    return lax.dot_general(a, b, (((0,), (0,)), ((), ())), preferred_element_type=F32)


def kernel(
    q_in, k_in, v_in, up_in, w_in,
    att_o, dq_o, dk_o, dv_o, wo_o,
    kv, held, qh, fu, wv, ust, uu, cg_acc, cgh, sc, nb, att_all, own, gs, gr, held_gr, part, wos, wor,
    loc, kv_s, kv_r, nk_s, nk_r, gr_s, gr_r, gn_s, gn_r, fy_s, fy_r, fc_s, fc_r, ua_s, ua_r, uy_s, uy_r, uc_s, uc_r,
    at_s, at_r, wo_s, wo_r,
):
    c = lax.axis_index("ctx")
    h = lax.axis_index("head")
    x = lax.div(c, ZS)
    z = lax.rem(c, ZS)
    core = lax.rem(h, 2)
    twin = h + 1 - 2 * core

    def at_ctx(shift):
        return (lax.rem(c + (shift + CTX), CTX), h)

    def at_z(shift):
        return (x * ZS + lax.rem(z + (shift + ZS), ZS), h)

    def at_head(shift):
        return (c, lax.rem(h + shift, HP))

    def cols(j, width):
        return pl.ds(pl.multiple_of(j * width, 128), width)

    def remote(src, dst, send, recv, device):
        return pltpu.make_async_remote_copy(
            src, dst, send, recv, device_id=device, device_id_type=MESH)

    def local_copy(kind, j):
        src = (k_in, v_in, q_in)[kind].at[:, j * HDIM : (j + 1) * HDIM]
        dst = qh.at[j] if kind == 2 else kv.at[j, kind, 0]
        return pltpu.make_async_copy(src, dst, loc.at[kind * HEADS + j])

    up_copy = pltpu.make_async_copy(up_in, fu.at[h], loc.at[12])
    w_copy = pltpu.make_async_copy(w_in, wv, loc.at[13])

    def kv_copy(lv, j, src=None):
        route, shift = KV_ROUTE[lv]
        return remote(
            kv.at[j, :, route if src is None else src], kv.at[j, :, lv],
            kv_s.at[lv - 1, j], kv_r.at[lv - 1, j], at_z(1) if lv == 1 else at_ctx(shift))

    def gr_copy(lv, j):
        return remote(
            gs.at[lv - 1, j], gr.at[lv - 1, j], gr_s.at[lv - 1, j], gr_r.at[lv - 1, j],
            at_ctx(-KV_ROUTE[lv][1]))

    def nk_copy(j, src):
        return remote(kv.at[j, :, src], held.at[j], nk_s.at[j], nk_r.at[j], at_z(-2))

    def nk_relay(j):
        return remote(held.at[j], kv.at[j, :, 3], kv_s.at[2, j], kv_r.at[2, j], at_z(-2))

    def gn_copy(j):
        return remote(gs.at[2, j], held_gr.at[j - 2], gn_s.at[j - 2], gn_r.at[j - 2], at_z(2))

    def gn_relay(j):
        return remote(held_gr.at[j - 2], gr.at[2, j], gr_s.at[2, j], gr_r.at[2, j], at_z(2))

    def from_y(s):
        return lax.rem(h + (HP - 2 * s), HP)

    def fy_copy(s):
        return remote(up_in, fu.at[h], fy_s.at[s], fy_r.at[s], at_head(2 * s))

    def fc_copy(s):
        slot = from_y(s)
        return remote(up_in if s == 0 else fu.at[slot], fu.at[slot], fc_s.at[s], fc_r.at[s], (c, twin))

    def ua_copy(s):
        return remote(ust.at[s], uu.at[h, x], ua_s.at[s], ua_r.at[s], at_ctx(s * ZS))

    def uy_copy(s):
        return remote(uu.at[h], uu.at[h], uy_s.at[s], uy_r.at[s], at_head(2 * s))

    def uc_copy(s):
        slot = from_y(s)
        return remote(uu.at[slot], uu.at[slot], uc_s.at[s], uc_r.at[s], (c, twin))

    def at_copy(s, j):
        piece = att_all.at[x, lax.div(j, 2), :, cols(lax.rem(j, 2), HDIM)]
        return remote(piece, piece, at_s.at[s, j], at_r.at[s, j], at_ctx(s * ZS))

    def wo_copy(g, way, k):
        return remote(
            wos.at[g, way, k], wor.at[g, way, k], wo_s.at[g, way, k], wo_r.at[g, way, k],
            at_z(1 - 2 * way))

    for j in range(HEADS):
        local_copy(0, j).start()
        local_copy(1, j).start()
    up_copy.start()
    for j in range(HEADS):
        local_copy(2, j).start()
    w_copy.start()

    barrier = pltpu.get_barrier_semaphore()
    peers = [at_ctx(shift) for shift in (1, -1, 2, -2, 8, 16, 24)]
    peers += [at_head(s) for s in (2, 4, 6)] + [(c, twin)]
    peers += [at_z(s) for s in (1, -1, 2, -2)]
    for peer in peers:
        pl.semaphore_signal(barrier, inc=1, device_id=peer, device_id_type=MESH)
    pl.semaphore_wait(barrier, len(peers))

    for s in range(1, XS):
        fy_copy(s).start()
    fc_copy(0).start()
    for j in range(HEADS):
        local_copy(0, j).wait()
        local_copy(1, j).wait()
        if j < 2:
            @pl.when(z < ZS - 1)
            def _():
                kv_copy(1, j).start()

            @pl.when(z < ZS // 2)
            def _():
                nk_copy(j, 0).start()

        kv_copy(4, j).start()

    def relay_near(j):
        kv_copy(4, j).wait_recv()
        kv_copy(5, j).start()

        @pl.when(z == ZS - 1)
        def _():
            kv_copy(1, j, 4).start()

        if j < 2:
            @pl.when(z >= ZS // 2)
            def _():
                nk_copy(j, 4).start()

        kv_copy(1, j).wait_recv()
        kv_copy(2, j).start()

        if j < 2:
            @pl.when(z < ZS - 1)
            def _():
                kv_copy(1, j + 2).start()

    def relay_down(j):
        nk_copy(j, 0).wait_recv()
        nk_relay(j).start()

    def relay_up(j):
        kv_copy(2, j).wait_recv()
        kv_copy(3, j).start()

    def pass_upstream():
        for s in range(1, XS):
            fy_copy(s).wait_recv()
            fc_copy(s).start()

    def exchange_columns():
        for s in range(XS):
            fc_copy(s).wait_recv()
        up_copy.wait()
        for s in range(XS):
            target = lax.rem(x + s, XS)
            tile = fu[2 * target + lax.div(h, 4), :, cols(lax.rem(h, 4), HDIM)].T
            if s == 0:
                uu[h, x] = tile
            else:
                ust[s] = tile
                ua_copy(s).start()

    def context():
        w_copy.wait()
        cg_acc[...] = dot_nt(fu[0], wv[:, 0:FEAT])

        def add_tile(tile, carry):
            cg_acc[...] += dot_nt(fu[tile], wv[:, cols(tile, FEAT)])
            return carry

        lax.fori_loop(1, HP, add_tile, 0)
        for j in range(HEADS):
            cgh[j] = cg_acc[:, j * HDIM : (j + 1) * HDIM].astype(BF16)
            local_copy(2, j).wait()

    def spread_columns():
        for s in range(1, XS):
            ua_copy(s).wait_recv()
        uc_copy(0).start()
        for s in range(1, XS):
            uy_copy(s).start()

    def finish_columns():
        for s in range(1, XS):
            uy_copy(s).wait_recv()
            uc_copy(s).start()
        for s in range(XS):
            uc_copy(s).wait_recv()

    def head(j):
        @pl.when(j < 2)
        def _():
            kv_copy(2, j).wait_recv()

        kv_copy(3, j).wait_recv()
        kv_copy(5, j).wait_recv()
        q = qh[j]
        cg = cgh[j]
        row_max = None
        for lv in range(LV):
            s = dot_nt(kv[j, 0, lv], q) * SCALING
            if lv == 0:
                key_id = lax.broadcasted_iota(jnp.int32, (BLK, BLK), 0)
                query_id = lax.broadcasted_iota(jnp.int32, (BLK, BLK), 1)
                s = jnp.where(key_id <= query_id, s, -1e30)
            else:
                s = s + jnp.where(c >= DISTANCES[lv], 0.0, -1e30).astype(F32)
            sc[lv] = s
            top = jnp.max(s, axis=0, keepdims=True)
            row_max = top if row_max is None else jnp.maximum(row_max, top)
        totals = jnp.zeros((1, BLK), F32)
        for lv in range(LV):
            w = jnp.exp(sc[lv] - row_max)
            sc[lv] = w
            totals = totals + jnp.sum(w, axis=0, keepdims=True)
            nb[lv * BLK : (lv + 1) * BLK, :] = w.astype(BF16)
        inverse = 1.0 / totals
        mixed = dot_tn(kv[j, 1].reshape(LV * BLK, HDIM), nb[...])
        att_t = (mixed * inverse).astype(BF16).astype(F32)
        att = att_t.T.astype(BF16)
        att_o[:, cols(j, HDIM)] = att
        att_all[x, lax.div(j, 2), :, cols(lax.rem(j, 2), HDIM)] = att
        for s in range(1, XS):
            at_copy(s, j).start()
        row_dots = jnp.sum(cg.astype(F32).T * att_t, axis=0, keepdims=True)
        for lv in (3, 5, 2, 4, 1, 0):
            normed = sc[lv] * inverse
            prob_grad = dot_nt(kv[j, 1, lv], cg)
            ds = (normed * (prob_grad - row_dots)).astype(BF16)
            nb[lv * BLK : (lv + 1) * BLK, :] = ds
            dv = dot_nn(normed.astype(BF16), cg)
            dk = dot_nn(ds, q) * SCALING
            if lv in (3, 5):
                gs[lv - 1, j, 0] = dk.astype(BF16)
                gs[lv - 1, j, 1] = dv.astype(BF16)
                if lv == 5:
                    gr_copy(lv, j).start()
                else:
                    @pl.when(j < RISE)
                    def _():
                        gr_copy(3, j).start()

                    @pl.when(j >= RISE)
                    def _():
                        gn_copy(j).start()
            else:
                own[lv, j, 0] = dk
                own[lv, j, 1] = dv
                if lv == 2:
                    @pl.when(j >= RISE)
                    def _():
                        gs[1, j, 0] = dk.astype(BF16)
                        gs[1, j, 1] = dv.astype(BF16)
                        gr_copy(2, j).start()
        dq_t = dot_tn(kv[j, 0].reshape(LV * BLK, HDIM), nb[...]) * SCALING
        dq_o[:, cols(j, HDIM)] = dq_t.T.astype(BF16)

    def pass_on(src, dst, j):
        gr_copy(src, j).wait_recv()
        gs[dst - 1, j] = (own[dst, j] + gr[src - 1, j].astype(F32)).astype(BF16)
        gr_copy(dst, j).start()

    def chain_one(j):
        pass_on(3, 2, j)

    def chain_two(j):
        pass_on(2, 1, j)

    def send_up(j):
        gn_copy(j).wait_recv()
        gn_relay(j).start()

    upper = (z >= ZS // 2).astype(F32)

    def eight(j):
        if j < RISE:
            pass_on(5, 4, j)
        else:
            gr_copy(5, j).wait_recv()
            gr_copy(3, j).wait_recv()
            total = own[4, j] + gr[4, j].astype(F32) + upper * gr[2, j].astype(F32)
            gs[3, j] = total.astype(BF16)
            gr_copy(4, j).start()

    def last(j):
        gr_copy(1, j).wait_recv()
        gr_copy(4, j).wait_recv()
        total = own[0, j] + gr[0, j].astype(F32) + gr[3, j].astype(F32)
        if j >= RISE:
            total = total + (1.0 - upper) * gr[2, j].astype(F32)
        dk_o[:, cols(j, HDIM)] = total[0].astype(BF16)
        dv_o[:, cols(j, HDIM)] = total[1].astype(BF16)

    def project(g):
        for j in (2 * g, 2 * g + 1):
            for s in range(1, XS):
                at_copy(s, j).wait_recv()

        def pieces(n, carry):
            rows = pl.ds(n * 4, 4)
            total = dot_nn(uu[rows, 0].reshape(4 * HDIM, BLK), att_all[0, g])
            for row in range(1, XS):
                total = total + dot_nn(uu[rows, row].reshape(4 * HDIM, BLK), att_all[row, g])
            part[g, rows] = total.reshape(4, HDIM, WIDE)
            return carry

        lax.fori_loop(0, ZS // 4, pieces, 0)
        for way, steps in ((0, UP), (1, DOWN)):
            wos[g, way, 0] = part[g, target_of(way, steps)].astype(BF16)
            wo_copy(g, way, 0).start()

    def target_of(way, left):
        return lax.rem(z + (left if way == 0 else ZS - left), ZS)

    def ring(g, k):
        for way, steps in ((0, UP), (1, DOWN)):
            if k > steps:
                continue
            wo_copy(g, way, k - 1).wait_recv()
            if k < steps:
                total = wor[g, way, k - 1].astype(F32) + part[g, target_of(way, steps - k)]
                wos[g, way, k] = total.astype(BF16)
                wo_copy(g, way, k).start()
            elif way == 1:
                part[g, z] = part[g, z] + wor[g, way, k - 1].astype(F32)
            else:
                wo_o[:, g * WIDE : (g + 1) * WIDE] = part[g, z] + wor[g, way, k - 1].astype(F32)

    relay_near(0)
    relay_near(1)
    relay_down(0)
    pass_upstream()
    relay_near(2)
    relay_down(1)
    exchange_columns()
    relay_near(3)
    context()
    relay_up(2)

    def stage(t, carry):
        @pl.when(t == 1)
        def _():
            spread_columns()
            relay_up(3)

        @pl.when(t == 3)
        def _():
            chain_one(0)

        head(t)
        return carry

    lax.fori_loop(0, HEADS, stage, 0)
    chain_one(1)
    send_up(2)
    finish_columns()
    project(1)
    project(0)
    eight(0)
    chain_two(0)
    eight(1)
    chain_two(1)
    ring(1, 1)
    ring(0, 1)
    send_up(3)
    chain_two(2)
    ring(1, 2)
    eight(2)
    ring(0, 2)
    eight(3)
    chain_two(3)
    ring(1, 3)
    ring(0, 3)
    last(2)
    last(1)
    last(0)
    ring(1, 4)
    last(3)
    ring(0, 4)

    def drain(j, carry):
        for lv in range(1, LV):
            kv_copy(lv, j).wait_send()
            gr_copy(lv, j).wait_send()
        for s in range(1, XS):
            at_copy(s, j).wait_send()
        return carry

    lax.fori_loop(0, HEADS, drain, 0)
    for j in (0, 1):
        nk_copy(j, 0).wait_send()
        if j + 2 >= RISE:
            gn_copy(j + 2).wait_send()
    for g in range(GROUPS):
        for way, steps in ((0, UP), (1, DOWN)):
            for k in range(steps):
                wo_copy(g, way, k).wait_send()
    fc_copy(0).wait_send()
    uc_copy(0).wait_send()
    for s in range(1, XS):
        fy_copy(s).wait_send()
        fc_copy(s).wait_send()
        ua_copy(s).wait_send()
        uy_copy(s).wait_send()
        uc_copy(s).wait_send()


def hand_over(*refs):
    copies = [pltpu.make_async_copy(refs[i], refs[5 + i], refs[10].at[i]) for i in range(5)]
    for copy in copies:
        copy.start()
    for copy in copies:
        copy.wait()


def per_device(queries, keys, values, upstream, out_weight):
    tokens = jax.ShapeDtypeStruct((BLK, FEAT), BF16)
    shapes = (tokens, tokens, tokens, tokens, jax.ShapeDtypeStruct((HDIM, FEAT), F32))
    dma = pltpu.SemaphoreType.DMA
    vmem = pltpu.VMEM
    results = pl.pallas_call(
        kernel,
        out_shape=shapes,
        in_specs=[pl.BlockSpec(memory_space=pl.ANY)] * 5,
        out_specs=(pl.BlockSpec(memory_space=pltpu.VMEM),) * 5,
        scratch_shapes=[
            vmem((HEADS, 2, LV, BLK, HDIM), BF16),
            vmem((2, 2, BLK, HDIM), BF16),
            vmem((HEADS, BLK, HDIM), BF16),
            vmem((HP, BLK, FEAT), BF16),
            vmem((FEAT, D), BF16),
            vmem((XS, HDIM, BLK), BF16),
            vmem((HP, XS, HDIM, BLK), BF16),
            vmem((BLK, FEAT), F32),
            vmem((HEADS, BLK, HDIM), BF16),
            vmem((LV, BLK, BLK), F32),
            vmem((LV * BLK, BLK), BF16),
            vmem((XS, GROUPS, BLK, WIDE), BF16),
            vmem((5, HEADS, 2, BLK, HDIM), F32),
            vmem((5, HEADS, 2, BLK, HDIM), BF16),
            vmem((5, HEADS, 2, BLK, HDIM), BF16),
            vmem((2, 2, BLK, HDIM), BF16),
            vmem((GROUPS, ZS, HDIM, WIDE), F32),
            vmem((GROUPS, 2, UP, HDIM, WIDE), BF16),
            vmem((GROUPS, 2, UP, HDIM, WIDE), BF16),
            dma((14,)),
            dma((5, HEADS)), dma((5, HEADS)),
            dma((2,)), dma((2,)),
            dma((5, HEADS)), dma((5, HEADS)),
            dma((2,)), dma((2,)),
            dma((XS,)), dma((XS,)), dma((XS,)), dma((XS,)),
            dma((XS,)), dma((XS,)),
            dma((XS,)), dma((XS,)), dma((XS,)), dma((XS,)),
            dma((XS, HEADS)), dma((XS, HEADS)),
            dma((GROUPS, 2, UP)), dma((GROUPS, 2, UP)),
        ],
        compiler_params=pltpu.CompilerParams(
            collective_id=0, has_side_effects=True, vmem_limit_bytes=52 * 1024 * 1024 + 512 * 1024
        ),
        cost_estimate=pl.CostEstimate(flops=5 * 10**9, bytes_accessed=10**7, transcendentals=2 * 10**6),
        name="log_sparse_attention",
    )(queries, keys, values, upstream, out_weight)
    return pl.pallas_call(
        hand_over,
        out_shape=shapes,
        in_specs=[pl.BlockSpec(memory_space=pltpu.VMEM)] * 5,
        out_specs=(pl.BlockSpec(memory_space=pl.ANY),) * 5,
        scratch_shapes=[dma((5,))],
        compiler_params=pltpu.CompilerParams(vmem_limit_bytes=4 * 1024 * 1024),
        name="hand_over",
    )(*results)


def solution(mesh):
    tiled = P("ctx", "head")
    return jax.shard_map(
        per_device,
        mesh=mesh,
        in_specs=(tiled, tiled, tiled, tiled, P("head", None)),
        out_specs=(tiled,) * 5,
        check_vma=False,
    )
```

```python
import math

import jax
import jax.numpy as jnp
from jax import lax
from jax.experimental import pallas as pl
from jax.experimental.pallas import tpu as pltpu
from jax.sharding import PartitionSpec as P

HDIM = 128
BLK = 256
DISTANCES = (0, 1, 2, 4, 8, 16)
LV = len(DISTANCES)
HEADS = 4
FEAT = HEADS * HDIM
D = 4096
CTX = 32
ZS = 8
XS = 4
UP = 4
DOWN = 3
RISE = 2
GROUPS = 2
WIDE = FEAT // GROUPS
HP = 8
SCALING = 1.0 / math.sqrt(HDIM)
MESH = pl.DeviceIdType.MESH
BF16 = jnp.bfloat16
F32 = jnp.float32

KV_ROUTE = {1: (0, 1), 2: (1, 1), 3: (2, 2), 4: (0, 8), 5: (4, 8)}


def dot_nt(a, b):
    return lax.dot_general(a, b, (((1,), (1,)), ((), ())), preferred_element_type=F32)


def dot_nn(a, b):
    return lax.dot_general(a, b, (((1,), (0,)), ((), ())), preferred_element_type=F32)


def dot_tn(a, b):
    return lax.dot_general(a, b, (((0,), (0,)), ((), ())), preferred_element_type=F32)


def kernel(
    q_in, k_in, v_in, up_in, w_in,
    att_o, dq_o, dk_o, dv_o, wo_o,
    kv, held, qh, fu, wv, ust, uu, cg_acc, cgh, sc, nb, att_all, own, gs, gr, held_gr, part, wos, wor,
    loc, kv_s, kv_r, nk_s, nk_r, gr_s, gr_r, gn_s, gn_r, fy_s, fy_r, fc_s, fc_r, ua_s, ua_r, uy_s, uy_r, uc_s, uc_r,
    at_s, at_r, wo_s, wo_r,
):
    c = lax.axis_index("ctx")
    h = lax.axis_index("head")
    x = lax.div(c, ZS)
    z = lax.rem(c, ZS)
    core = lax.rem(h, 2)
    twin = h + 1 - 2 * core

    def at_ctx(shift):
        return (lax.rem(c + (shift + CTX), CTX), h)

    def at_z(shift):
        return (x * ZS + lax.rem(z + (shift + ZS), ZS), h)

    def at_head(shift):
        return (c, lax.rem(h + shift, HP))

    def cols(j, width):
        return pl.ds(pl.multiple_of(j * width, 128), width)

    def remote(src, dst, send, recv, device):
        return pltpu.make_async_remote_copy(
            src, dst, send, recv, device_id=device, device_id_type=MESH)

    def local_copy(kind, j):
        src = (k_in, v_in, q_in)[kind].at[:, j * HDIM : (j + 1) * HDIM]
        dst = qh.at[j] if kind == 2 else kv.at[j, kind, 0]
        return pltpu.make_async_copy(src, dst, loc.at[kind * HEADS + j])

    up_copy = pltpu.make_async_copy(up_in, fu.at[h], loc.at[12])
    w_copy = pltpu.make_async_copy(w_in, wv, loc.at[13])

    def kv_copy(lv, j, src=None):
        route, shift = KV_ROUTE[lv]
        return remote(
            kv.at[j, :, route if src is None else src], kv.at[j, :, lv],
            kv_s.at[lv - 1, j], kv_r.at[lv - 1, j], at_z(1) if lv == 1 else at_ctx(shift))

    def gr_copy(lv, j):
        return remote(
            gs.at[lv - 1, j], gr.at[lv - 1, j], gr_s.at[lv - 1, j], gr_r.at[lv - 1, j],
            at_ctx(-KV_ROUTE[lv][1]))

    def nk_copy(j, src):
        return remote(kv.at[j, :, src], held.at[j], nk_s.at[j], nk_r.at[j], at_z(-2))

    def nk_relay(j):
        return remote(held.at[j], kv.at[j, :, 3], kv_s.at[2, j], kv_r.at[2, j], at_z(-2))

    def gn_copy(j):
        return remote(gs.at[2, j], held_gr.at[j - 2], gn_s.at[j - 2], gn_r.at[j - 2], at_z(2))

    def gn_relay(j):
        return remote(held_gr.at[j - 2], gr.at[2, j], gr_s.at[2, j], gr_r.at[2, j], at_z(2))

    def from_y(s):
        return lax.rem(h + (HP - 2 * s), HP)

    def fy_copy(s):
        return remote(up_in, fu.at[h], fy_s.at[s], fy_r.at[s], at_head(2 * s))

    def fc_copy(s):
        slot = from_y(s)
        return remote(up_in if s == 0 else fu.at[slot], fu.at[slot], fc_s.at[s], fc_r.at[s], (c, twin))

    def ua_copy(s):
        return remote(ust.at[s], uu.at[h, x], ua_s.at[s], ua_r.at[s], at_ctx(s * ZS))

    def uy_copy(s):
        return remote(uu.at[h], uu.at[h], uy_s.at[s], uy_r.at[s], at_head(2 * s))

    def uc_copy(s):
        slot = from_y(s)
        return remote(uu.at[slot], uu.at[slot], uc_s.at[s], uc_r.at[s], (c, twin))

    def at_copy(s, j):
        piece = att_all.at[x, lax.div(j, 2), :, cols(lax.rem(j, 2), HDIM)]
        return remote(piece, piece, at_s.at[s, j], at_r.at[s, j], at_ctx(s * ZS))

    def wo_copy(g, way, k):
        return remote(
            wos.at[g, way, k], wor.at[g, way, k], wo_s.at[g, way, k], wo_r.at[g, way, k],
            at_z(1 - 2 * way))

    for j in range(HEADS):
        local_copy(0, j).start()
        local_copy(1, j).start()
    up_copy.start()
    for j in range(HEADS):
        local_copy(2, j).start()
    w_copy.start()

    barrier = pltpu.get_barrier_semaphore()
    peers = [at_ctx(shift) for shift in (1, -1, 2, -2, 8, 16, 24)]
    peers += [at_head(s) for s in (2, 4, 6)] + [(c, twin)]
    peers += [at_z(s) for s in (1, -1, 2, -2)]
    for peer in peers:
        pl.semaphore_signal(barrier, inc=1, device_id=peer, device_id_type=MESH)
    pl.semaphore_wait(barrier, len(peers))

    for s in range(1, XS):
        fy_copy(s).start()
    fc_copy(0).start()
    for j in range(HEADS):
        local_copy(0, j).wait()
        local_copy(1, j).wait()
        if j < 2:
            @pl.when(z < ZS - 1)
            def _():
                kv_copy(1, j).start()

            @pl.when(z < ZS // 2)
            def _():
                nk_copy(j, 0).start()

        kv_copy(4, j).start()

    def relay_near(j):
        kv_copy(4, j).wait_recv()
        kv_copy(5, j).start()

        @pl.when(z == ZS - 1)
        def _():
            kv_copy(1, j, 4).start()

        if j < 2:
            @pl.when(z >= ZS // 2)
            def _():
                nk_copy(j, 4).start()

        kv_copy(1, j).wait_recv()
        kv_copy(2, j).start()

        if j < 2:
            @pl.when(z < ZS - 1)
            def _():
                kv_copy(1, j + 2).start()

    def relay_down(j):
        nk_copy(j, 0).wait_recv()
        nk_relay(j).start()

    def relay_up(j):
        kv_copy(2, j).wait_recv()
        kv_copy(3, j).start()

    def pass_upstream():
        for s in range(1, XS):
            fy_copy(s).wait_recv()
            fc_copy(s).start()

    def exchange_columns():
        for s in range(XS):
            fc_copy(s).wait_recv()
        up_copy.wait()
        for s in range(XS):
            target = lax.rem(x + s, XS)
            tile = fu[2 * target + lax.div(h, 4), :, cols(lax.rem(h, 4), HDIM)].T
            if s == 0:
                uu[h, x] = tile
            else:
                ust[s] = tile
                ua_copy(s).start()

    def context():
        w_copy.wait()
        cg_acc[...] = dot_nt(fu[0], wv[:, 0:FEAT])

        def add_tile(tile, carry):
            cg_acc[...] += dot_nt(fu[tile], wv[:, cols(tile, FEAT)])
            return carry

        lax.fori_loop(1, HP, add_tile, 0)
        for j in range(HEADS):
            cgh[j] = cg_acc[:, j * HDIM : (j + 1) * HDIM].astype(BF16)
            local_copy(2, j).wait()

    def spread_columns():
        for s in range(1, XS):
            ua_copy(s).wait_recv()
        uc_copy(0).start()
        for s in range(1, XS):
            uy_copy(s).start()

    def finish_columns():
        for s in range(1, XS):
            uy_copy(s).wait_recv()
            uc_copy(s).start()
        for s in range(XS):
            uc_copy(s).wait_recv()

    def head(j):
        @pl.when(j < 2)
        def _():
            kv_copy(2, j).wait_recv()

        kv_copy(3, j).wait_recv()
        kv_copy(5, j).wait_recv()
        q = qh[j]
        cg = cgh[j]
        row_max = None
        for lv in range(LV):
            s = dot_nt(kv[j, 0, lv], q) * SCALING
            if lv == 0:
                key_id = lax.broadcasted_iota(jnp.int32, (BLK, BLK), 0)
                query_id = lax.broadcasted_iota(jnp.int32, (BLK, BLK), 1)
                s = jnp.where(key_id <= query_id, s, -1e30)
            else:
                s = s + jnp.where(c >= DISTANCES[lv], 0.0, -1e30).astype(F32)
            sc[lv] = s
            top = jnp.max(s, axis=0, keepdims=True)
            row_max = top if row_max is None else jnp.maximum(row_max, top)
        totals = jnp.zeros((1, BLK), F32)
        for lv in range(LV):
            w = jnp.exp(sc[lv] - row_max)
            sc[lv] = w
            totals = totals + jnp.sum(w, axis=0, keepdims=True)
            nb[lv * BLK : (lv + 1) * BLK, :] = w.astype(BF16)
        inverse = 1.0 / totals
        mixed = dot_tn(kv[j, 1].reshape(LV * BLK, HDIM), nb[...])
        att_t = (mixed * inverse).astype(BF16).astype(F32)
        att = att_t.T.astype(BF16)
        att_o[:, cols(j, HDIM)] = att
        att_all[x, lax.div(j, 2), :, cols(lax.rem(j, 2), HDIM)] = att
        for s in range(1, XS):
            at_copy(s, j).start()
        row_dots = jnp.sum(cg.astype(F32).T * att_t, axis=0, keepdims=True)
        for lv in (3, 5, 2, 4, 1, 0):
            normed = sc[lv] * inverse
            prob_grad = dot_nt(kv[j, 1, lv], cg)
            ds = (normed * (prob_grad - row_dots)).astype(BF16)
            nb[lv * BLK : (lv + 1) * BLK, :] = ds
            dv = dot_nn(normed.astype(BF16), cg)
            dk = dot_nn(ds, q) * SCALING
            if lv in (3, 5):
                gs[lv - 1, j, 0] = dk.astype(BF16)
                gs[lv - 1, j, 1] = dv.astype(BF16)
                if lv == 5:
                    gr_copy(lv, j).start()
                else:
                    @pl.when(j < RISE)
                    def _():
                        gr_copy(3, j).start()

                    @pl.when(j >= RISE)
                    def _():
                        gn_copy(j).start()
            else:
                own[lv, j, 0] = dk
                own[lv, j, 1] = dv
                if lv == 2:
                    @pl.when(j >= RISE)
                    def _():
                        gs[1, j, 0] = dk.astype(BF16)
                        gs[1, j, 1] = dv.astype(BF16)
                        gr_copy(2, j).start()
        dq_t = dot_tn(kv[j, 0].reshape(LV * BLK, HDIM), nb[...]) * SCALING
        dq_o[:, cols(j, HDIM)] = dq_t.T.astype(BF16)

    def pass_on(src, dst, j):
        gr_copy(src, j).wait_recv()
        gs[dst - 1, j] = (own[dst, j] + gr[src - 1, j].astype(F32)).astype(BF16)
        gr_copy(dst, j).start()

    def chain_one(j):
        pass_on(3, 2, j)

    def chain_two(j):
        pass_on(2, 1, j)

    def send_up(j):
        gn_copy(j).wait_recv()
        gn_relay(j).start()

    upper = (z >= ZS // 2).astype(F32)

    def eight(j):
        if j < RISE:
            pass_on(5, 4, j)
        else:
            gr_copy(5, j).wait_recv()
            gr_copy(3, j).wait_recv()
            total = own[4, j] + gr[4, j].astype(F32) + upper * gr[2, j].astype(F32)
            gs[3, j] = total.astype(BF16)
            gr_copy(4, j).start()

    def last(j):
        gr_copy(1, j).wait_recv()
        gr_copy(4, j).wait_recv()
        total = own[0, j] + gr[0, j].astype(F32) + gr[3, j].astype(F32)
        if j >= RISE:
            total = total + (1.0 - upper) * gr[2, j].astype(F32)
        dk_o[:, cols(j, HDIM)] = total[0].astype(BF16)
        dv_o[:, cols(j, HDIM)] = total[1].astype(BF16)

    def project(g):
        for j in (2 * g, 2 * g + 1):
            for s in range(1, XS):
                at_copy(s, j).wait_recv()

        def pieces(n, carry):
            rows = pl.ds(n * 4, 4)
            total = dot_nn(uu[rows, 0].reshape(4 * HDIM, BLK), att_all[0, g])
            for row in range(1, XS):
                total = total + dot_nn(uu[rows, row].reshape(4 * HDIM, BLK), att_all[row, g])
            part[g, rows] = total.reshape(4, HDIM, WIDE)
            return carry

        lax.fori_loop(0, ZS // 4, pieces, 0)
        for way, steps in ((0, UP), (1, DOWN)):
            wos[g, way, 0] = part[g, target_of(way, steps)].astype(BF16)
            wo_copy(g, way, 0).start()

    def target_of(way, left):
        return lax.rem(z + (left if way == 0 else ZS - left), ZS)

    def ring(g, k):
        for way, steps in ((0, UP), (1, DOWN)):
            if k > steps:
                continue
            wo_copy(g, way, k - 1).wait_recv()
            if k < steps:
                total = wor[g, way, k - 1].astype(F32) + part[g, target_of(way, steps - k)]
                wos[g, way, k] = total.astype(BF16)
                wo_copy(g, way, k).start()
            elif way == 1:
                part[g, z] = part[g, z] + wor[g, way, k - 1].astype(F32)
            else:
                wo_o[:, g * WIDE : (g + 1) * WIDE] = part[g, z] + wor[g, way, k - 1].astype(F32)

    relay_near(0)
    relay_near(1)
    relay_down(0)
    pass_upstream()
    relay_near(2)
    relay_down(1)
    exchange_columns()
    relay_near(3)
    context()
    relay_up(2)

    def stage(t, carry):
        @pl.when(t == 1)
        def _():
            spread_columns()
            relay_up(3)

        @pl.when(t == 3)
        def _():
            chain_one(0)

        head(t)
        return carry

    lax.fori_loop(0, HEADS, stage, 0)
    chain_one(1)
    eight(0)
    send_up(2)
    finish_columns()
    chain_two(0)
    project(1)
    project(0)
    chain_two(1)
    ring(1, 1)
    ring(0, 1)
    send_up(3)
    eight(1)
    eight(2)
    chain_two(2)
    ring(0, 2)
    ring(1, 2)
    chain_two(3)
    last(0)
    eight(3)
    last(2)
    ring(0, 3)
    ring(1, 3)
    last(1)
    ring(0, 4)
    last(3)
    ring(1, 4)

    def drain(j, carry):
        for lv in range(1, LV):
            kv_copy(lv, j).wait_send()
            gr_copy(lv, j).wait_send()
        for s in range(1, XS):
            at_copy(s, j).wait_send()
        return carry

    lax.fori_loop(0, HEADS, drain, 0)
    for j in (0, 1):
        nk_copy(j, 0).wait_send()
        if j + 2 >= RISE:
            gn_copy(j + 2).wait_send()
    for g in range(GROUPS):
        for way, steps in ((0, UP), (1, DOWN)):
            for k in range(steps):
                wo_copy(g, way, k).wait_send()
    fc_copy(0).wait_send()
    uc_copy(0).wait_send()
    for s in range(1, XS):
        fy_copy(s).wait_send()
        fc_copy(s).wait_send()
        ua_copy(s).wait_send()
        uy_copy(s).wait_send()
        uc_copy(s).wait_send()


def hand_over(*refs):
    copies = [pltpu.make_async_copy(refs[i], refs[5 + i], refs[10].at[i]) for i in range(5)]
    for copy in copies:
        copy.start()
    for copy in copies:
        copy.wait()


def per_device(queries, keys, values, upstream, out_weight):
    tokens = jax.ShapeDtypeStruct((BLK, FEAT), BF16)
    shapes = (tokens, tokens, tokens, tokens, jax.ShapeDtypeStruct((HDIM, FEAT), F32))
    dma = pltpu.SemaphoreType.DMA
    vmem = pltpu.VMEM
    results = pl.pallas_call(
        kernel,
        out_shape=shapes,
        in_specs=[pl.BlockSpec(memory_space=pl.ANY)] * 5,
        out_specs=(pl.BlockSpec(memory_space=pltpu.VMEM),) * 5,
        scratch_shapes=[
            vmem((HEADS, 2, LV, BLK, HDIM), BF16),
            vmem((2, 2, BLK, HDIM), BF16),
            vmem((HEADS, BLK, HDIM), BF16),
            vmem((HP, BLK, FEAT), BF16),
            vmem((FEAT, D), BF16),
            vmem((XS, HDIM, BLK), BF16),
            vmem((HP, XS, HDIM, BLK), BF16),
            vmem((BLK, FEAT), F32),
            vmem((HEADS, BLK, HDIM), BF16),
            vmem((LV, BLK, BLK), F32),
            vmem((LV * BLK, BLK), BF16),
            vmem((XS, GROUPS, BLK, WIDE), BF16),
            vmem((5, HEADS, 2, BLK, HDIM), F32),
            vmem((5, HEADS, 2, BLK, HDIM), BF16),
            vmem((5, HEADS, 2, BLK, HDIM), BF16),
            vmem((2, 2, BLK, HDIM), BF16),
            vmem((GROUPS, ZS, HDIM, WIDE), F32),
            vmem((GROUPS, 2, UP, HDIM, WIDE), BF16),
            vmem((GROUPS, 2, UP, HDIM, WIDE), BF16),
            dma((14,)),
            dma((5, HEADS)), dma((5, HEADS)),
            dma((2,)), dma((2,)),
            dma((5, HEADS)), dma((5, HEADS)),
            dma((2,)), dma((2,)),
            dma((XS,)), dma((XS,)), dma((XS,)), dma((XS,)),
            dma((XS,)), dma((XS,)),
            dma((XS,)), dma((XS,)), dma((XS,)), dma((XS,)),
            dma((XS, HEADS)), dma((XS, HEADS)),
            dma((GROUPS, 2, UP)), dma((GROUPS, 2, UP)),
        ],
        compiler_params=pltpu.CompilerParams(
            collective_id=0, has_side_effects=True, vmem_limit_bytes=52 * 1024 * 1024 + 512 * 1024
        ),
        cost_estimate=pl.CostEstimate(flops=5 * 10**9, bytes_accessed=10**7, transcendentals=2 * 10**6),
        name="log_sparse_attention",
    )(queries, keys, values, upstream, out_weight)
    return pl.pallas_call(
        hand_over,
        out_shape=shapes,
        in_specs=[pl.BlockSpec(memory_space=pltpu.VMEM)] * 5,
        out_specs=(pl.BlockSpec(memory_space=pl.ANY),) * 5,
        scratch_shapes=[dma((5,))],
        compiler_params=pltpu.CompilerParams(vmem_limit_bytes=4 * 1024 * 1024),
        name="hand_over",
    )(*results)


def solution(mesh):
    tiled = P("ctx", "head")
    return jax.shard_map(
        per_device,
        mesh=mesh,
        in_specs=(tiled, tiled, tiled, tiled, P("head", None)),
        out_specs=(tiled,) * 5,
        check_vma=False,
    )
```
